512 devices in a mesh: dp: 4 (over y), ctx: 4 (over x), expert: 32 (over z, core).
Axes of the slice: x: 4, y: 4, z: 16, core: 2. Of those that a mesh axis runs over, the one named last changes fastest.
Arguments:
- query_rows: bfloat16 [4, 4, 32, 256, 2048], P('dp', 'ctx', 'expert'), may hold values from -7 to 7
- key_rows: bfloat16 [4, 4, 32, 256, 256], P('dp', 'ctx', 'expert'), may hold values from -7 to 7
- value_rows: bfloat16 [4, 4, 32, 256, 256], P('dp', 'ctx', 'expert'), may hold values from -6 to 6
- output_grad: bfloat16 [4, 4, 32, 256, 2048], P('dp', 'ctx', 'expert'), may hold values from -6 to 6
- sink_logits: float32 [32], replicated, may hold values from -1 to 2
- parent_branch: int32 [4, 4, 32], P('dp', 'ctx', 'expert'), may hold values from 0 to 31, as said below
- segment_length: int32 [4, 4, 32], P('dp', 'ctx', 'expert'), may hold values from 128 to 256
Outputs:
- query_grad: bfloat16 [4, 4, 32, 256, 2048], P('dp', 'ctx', 'expert')
- key_grad: bfloat16 [4, 4, 32, 256, 256], P('dp', 'ctx', 'expert')
- value_grad: bfloat16 [4, 4, 32, 256, 256], P('dp', 'ctx', 'expert')
- sink_grad: float32 [32], replicated
The draws below stay inside these ranges and needn't reach their ends.
Inputs may be any that keep to these rules, and one draw needn't show every extreme that they name: parent_branch[t, l, b] lies in b - 1 .. b + 1; entries of level 0 are not read.
All inputs are finite; a program needn't handle non-finite values.
Results may differ from the reference program's by a relative error of at most 0.0034.
The reference program's roundings to bfloat16 on the way count: a program that leaves them out, or rounds other values in their place, can miss the bound.
Values may be sent and summed in bfloat16 or wider, within the bound.
No kernel may reach another device: no remote copies, remote signals or barrier semaphores. Data moves between devices by JAX's collectives and lax.ppermute only.
A program may use at most 64 MiB of HBM per device.

```python
import jax
import jax.numpy as jnp
from jax import lax

HQ = 32
HK = 4
HD = 64
WIN = 128
TOK_DEV = 256
TREES = 4
LEVELS = 4
BRANCHES = 32


def draw_query_rows(key, part):
    key = jax.random.fold_in(key, 7)
    jitter_key = jax.random.fold_in(key, 0)
    full_shape = (TREES, LEVELS, BRANCHES, TOK_DEV, HQ, HD)
    drawn_rows = jnp.clip(jax.random.normal(jitter_key, full_shape, jnp.float32), -6.0, 6.0)
    return drawn_rows.reshape(TREES, LEVELS, BRANCHES, TOK_DEV, HQ * HD).astype(jnp.bfloat16)


def draw_key_rows(key, part):
    key = jax.random.fold_in(key, 13)
    jitter_key = jax.random.fold_in(key, 0)
    full_shape = (TREES, LEVELS, BRANCHES, TOK_DEV, HK, HD)
    drawn_rows = jnp.clip(jax.random.normal(jitter_key, full_shape, jnp.float32), -6.0, 6.0)
    return drawn_rows.reshape(TREES, LEVELS, BRANCHES, TOK_DEV, HK * HD).astype(jnp.bfloat16)


def draw_parent_branch(key, part):
    key = jax.random.fold_in(key, 5)
    branch_step = jax.random.randint(key, (TREES, LEVELS, BRANCHES), -1, 2)
    branch = jnp.arange(BRANCHES, dtype=jnp.int32)[None, None, :]
    return jnp.clip(branch + branch_step, 0, BRANCHES - 1).astype(jnp.int32)


def set_ends(array, stream_key, least, high):
    place = [jax.random.randint(jax.random.fold_in(stream_key, axis), (), 0, length) for axis, length in enumerate(array.shape)]
    longest = array.shape.index(max(array.shape))
    neighbour = place[:longest] + [(place[longest] + 1) % array.shape[longest]] + place[longest + 1:]
    return array.at[tuple(place)].set(least).at[tuple(neighbour)].set(high)


def level_of(stream_key, extent, shards, low, largest):
    loudness = 1.0
    for axis_at, blocks in shards:
        heights = jax.random.uniform(jax.random.fold_in(jax.random.fold_in(stream_key, 6), axis_at), (blocks,), jnp.float32, low / len(shards), largest / len(shards))
        loudness = loudness * jnp.repeat(jnp.exp(heights), extent[axis_at] // blocks).reshape((-1,) + (1,) * (len(extent) - 1 - axis_at))
    return loudness


def centred(stream_key, extent, spread, limit, cuts=(), held_as=jnp.bfloat16):
    level = level_of(stream_key, extent, cuts, -0.22, 0.18) if cuts else 1.0
    array = jax.random.normal(stream_key, extent, jnp.float32) * spread * level
    return jnp.minimum(jnp.maximum(array, -limit), limit).astype(held_as)


def setup_inputs(seed: int = 0) -> dict:
    key_of = jax.random.split(jax.random.key(seed), 8)
    query_rows = draw_query_rows(jax.random.fold_in(key_of[7], 71), 0)
    key_rows = draw_key_rows(jax.random.fold_in(key_of[7], 71), 0)
    value_rows = centred(key_of[2], (TREES, LEVELS, BRANCHES, TOK_DEV, HK * HD), 1.0, 6.0, ((0, 4), (1, 4), (2, 32)))
    output_grad = centred(key_of[3], (TREES, LEVELS, BRANCHES, TOK_DEV, HQ * HD), 1.0, 6.0, ((0, 4), (1, 4), (2, 32)))
    sink_logits = jnp.clip(jax.random.uniform(key_of[4], (HQ,), jnp.float32, -1.0, 2.0), -1.0, 2.0)
    parent_branch = draw_parent_branch(jax.random.fold_in(key_of[7], 71), 0)
    segment_length = set_ends(jax.random.randint(key_of[6], (TREES, LEVELS, BRANCHES), WIN, TOK_DEV + 1), jax.random.fold_in(key_of[6], 1), WIN, TOK_DEV).astype(jnp.int32)
    return dict(query_rows=query_rows, key_rows=key_rows, value_rows=value_rows, output_grad=output_grad, sink_logits=sink_logits, parent_branch=parent_branch, segment_length=segment_length)


def attend_backward(query_rows, key_rows, value_rows, output_grad, tail_keys, tail_values, live_count, has_parent, sink_logits):
    tokens = query_rows.shape[0]
    tail_len = tail_keys.shape[0]
    group_size = HQ // HK
    score_scale = HD ** -0.5
    row_index = jnp.arange(tokens, dtype=jnp.int32)[:, None]
    col_index = jnp.arange(tail_len + tokens, dtype=jnp.int32)[None, :]
    own_col = col_index - tail_len
    in_tail = (col_index < tail_len) & (col_index >= row_index) & has_parent
    in_own = (col_index >= tail_len) & (own_col <= row_index) & (own_col > row_index - WIN)
    visible = (in_tail | in_own) & (row_index < live_count)
    all_keys = jnp.concatenate([tail_keys, key_rows], axis=0)
    all_values = jnp.concatenate([tail_values, value_rows], axis=0)
    query_parts, key_parts, value_parts, sink_parts = [], [], [], []
    for head_group in range(HK):
        first_col = head_group * group_size * HD
        last_col = first_col + group_size * HD
        grouped_q = query_rows[:, first_col:last_col].reshape(tokens, group_size, HD).astype(jnp.float32)
        grouped_d = output_grad[:, first_col:last_col].reshape(tokens, group_size, HD).astype(jnp.float32)
        group_keys = all_keys[:, head_group * HD:(head_group + 1) * HD].astype(jnp.float32)
        group_values = all_values[:, head_group * HD:(head_group + 1) * HD].astype(jnp.float32)
        group_sinks = sink_logits[head_group * group_size:(head_group + 1) * group_size]
        scores = jnp.einsum("ihd,jd->hij", grouped_q, group_keys) * score_scale
        scores = jnp.where(visible[None], scores, -1e30)
        row_max = jnp.maximum(jnp.max(scores, axis=2), group_sinks[:, None])
        weights = jnp.exp(scores - row_max[:, :, None])
        sink_weight = jnp.exp(group_sinks[:, None] - row_max)
        denominator = jnp.sum(weights, axis=2) + sink_weight
        probabilities = weights / denominator[:, :, None]
        sink_prob = sink_weight / denominator
        probs_low = probabilities.astype(jnp.bfloat16).astype(jnp.float32)
        outputs = jnp.einsum("hij,jd->hid", probs_low, group_values)
        row_delta = jnp.sum(outputs * jnp.swapaxes(grouped_d, 0, 1), axis=2)
        dot_grad = jnp.einsum("ihd,jd->hij", grouped_d, group_values)
        score_grad = (probabilities * (dot_grad - row_delta[:, :, None])).astype(jnp.bfloat16).astype(jnp.float32)
        query_parts.append((jnp.einsum("hij,jd->ihd", score_grad, group_keys) * score_scale).reshape(tokens, group_size * HD))
        key_parts.append(jnp.einsum("hij,ihd->jd", score_grad, grouped_q) * score_scale)
        value_parts.append(jnp.einsum("hij,ihd->jd", probs_low, grouped_d))
        sink_parts.append(-jnp.sum(sink_prob * row_delta, axis=1))
    query_grad = jnp.concatenate(query_parts, axis=1).astype(jnp.bfloat16)
    return query_grad, jnp.concatenate(key_parts, axis=1), jnp.concatenate(value_parts, axis=1), jnp.concatenate(sink_parts, axis=0)


def reference(query_rows, key_rows, value_rows, output_grad, sink_logits, parent_branch, segment_length):
    tail_len = WIN - 1
    segments = TREES * LEVELS * BRANCHES
    width_kv = HK * HD
    live_counts = segment_length.reshape(segments).astype(jnp.int32)

    def tail_of(source_rows, live_count):
        return lax.dynamic_slice_in_dim(source_rows, (live_count - tail_len).astype(jnp.int32), tail_len, 0)

    flat_q = query_rows.reshape(segments, TOK_DEV, HQ * HD)
    flat_d = output_grad.reshape(segments, TOK_DEV, HQ * HD)
    flat_keys = key_rows.reshape(segments, TOK_DEV, width_kv)
    flat_values = value_rows.reshape(segments, TOK_DEV, width_kv)
    chosen_index = jnp.broadcast_to(parent_branch[:, 1:, :, None, None].astype(jnp.int32), (TREES, LEVELS - 1, BRANCHES, tail_len, width_kv))
    empty_level = jnp.zeros((TREES, 1, BRANCHES, tail_len, width_kv), jnp.bfloat16)

    def parent_tails(flat_rows):
        tails = jax.vmap(tail_of)(flat_rows, live_counts).reshape(TREES, LEVELS, BRANCHES, tail_len, width_kv)
        picked = jnp.take_along_axis(tails[:, :-1], chosen_index, axis=2)
        return jnp.concatenate([empty_level, picked], axis=1).reshape(segments, tail_len, width_kv)

    parent_keys = parent_tails(flat_keys)
    parent_values = parent_tails(flat_values)
    has_parent = jnp.broadcast_to((jnp.arange(LEVELS) > 0)[None, :, None], (TREES, LEVELS, BRANCHES)).reshape(segments)

    def one_segment(inputs):
        return attend_backward(*inputs, sink_logits)

    query_grad, key_all, value_all, sink_terms = lax.map(one_segment, (flat_q, flat_keys, flat_values, flat_d, parent_keys, parent_values, live_counts, has_parent))
    selector = (parent_branch[:, 1:, :, None] == jnp.arange(BRANCHES, dtype=jnp.int32)[None, None, None, :]).astype(jnp.float32)

    def to_parents(all_rows):
        rounded = lax.optimization_barrier(all_rows[:, :tail_len].astype(jnp.bfloat16)).astype(jnp.float32)
        child_part = rounded.reshape(TREES, LEVELS, BRANCHES, tail_len, width_kv)[:, 1:]
        summed = jnp.einsum("tcep,tcewd->tcpwd", selector, child_part, precision=lax.Precision.HIGHEST)
        summed = jnp.concatenate([summed, jnp.zeros((TREES, 1, BRANCHES, tail_len, width_kv), jnp.float32)], axis=1)
        summed = summed.reshape(segments, tail_len, width_kv)
        placed = jax.vmap(lambda base_rows, extra_rows, live_count: lax.dynamic_update_slice_in_dim(base_rows, extra_rows, (live_count - tail_len).astype(jnp.int32), 0))(jnp.zeros((segments, TOK_DEV, width_kv), jnp.float32), summed, live_counts)
        return (all_rows[:, tail_len:] + placed).astype(jnp.bfloat16).reshape(TREES, LEVELS, BRANCHES, TOK_DEV, width_kv)

    key_grad = to_parents(key_all)
    value_grad = to_parents(value_all)
    query_grad = query_grad.reshape(TREES, LEVELS, BRANCHES, TOK_DEV, HQ * HD)
    sink_grad = jnp.sum(sink_terms, axis=0)
    return query_grad, key_grad, value_grad, sink_grad
```

```python
import jax
import jax.numpy as jnp
from jax import lax
from jax.sharding import PartitionSpec as P

HQ = 32
HK = 4
HD = 64
WIN = 128


def passed_along(shard, axis, by):
    peers = lax.axis_size(axis)
    pairs = [(i, i + by) for i in range(peers) if 0 <= i + by < peers]
    return lax.ppermute(shard, axis, pairs)


def summed_over(terms, axes):
    peers = 1
    for axis in axes:
        peers *= lax.axis_size(axis)
    copies = jnp.broadcast_to(terms[None], (peers,) + terms.shape)
    return jnp.sum(lax.all_to_all(copies, axes, 0, 0, tiled=True), axis=0)


def padded(cells, sides, width):
    for axis, dim in sides:
        count = lax.axis_size(axis)
        ends = count - 1
        head = lax.slice_in_dim(cells, 0, width, axis=dim)
        tail = lax.slice_in_dim(cells, cells.shape[dim] - width, cells.shape[dim], axis=dim)
        cells = jnp.concatenate(
            [
                lax.ppermute(tail, axis, [(i, (i + 1) % count) for i in range(ends)]),
                cells,
                lax.ppermute(head, axis, [((i + 1) % count, i) for i in range(ends)]),
            ],
            axis=dim,
        )
    return cells


def attend_backward(
    query_rows,
    key_rows,
    value_rows,
    output_grad,
    tail_keys,
    tail_values,
    live_count,
    has_parent,
    sink_logits,
):
    tokens = query_rows.shape[0]
    tail_len = tail_keys.shape[0]
    group_size = HQ // HK
    score_scale = HD ** (-0.5)
    row_index = jnp.arange(tokens, dtype=jnp.int32)[:, None]
    col_index = jnp.arange(tail_len + tokens, dtype=jnp.int32)[None, :]
    own_col = col_index - tail_len
    in_tail = (col_index < tail_len) & (col_index >= row_index) & has_parent
    in_own = (col_index >= tail_len) & (own_col <= row_index) & (own_col > row_index - WIN)
    visible = (in_tail | in_own) & (row_index < live_count)
    all_keys = jnp.concatenate([tail_keys, key_rows], axis=0)
    all_values = jnp.concatenate([tail_values, value_rows], axis=0)
    query_parts, key_parts, value_parts, sink_parts = ([], [], [], [])
    for head_group in range(HK):
        first_col = head_group * group_size * HD
        last_col = first_col + group_size * HD
        grouped_q = query_rows[:, first_col:last_col].reshape(tokens, group_size, HD)
        grouped_d = output_grad[:, first_col:last_col].reshape(tokens, group_size, HD)
        group_keys = all_keys[:, head_group * HD : (head_group + 1) * HD]
        group_values = all_values[:, head_group * HD : (head_group + 1) * HD]
        group_sinks = sink_logits[head_group * group_size : (head_group + 1) * group_size]
        scores = (
            jnp.einsum("ihd,jd->hij", grouped_q, group_keys, preferred_element_type=jnp.float32)
            * score_scale
        )
        scores = jnp.where(visible[None], scores, -1e30)
        row_max = jnp.maximum(jnp.max(scores, axis=2), group_sinks[:, None])
        weights = jnp.exp(scores - row_max[:, :, None])
        sink_weight = jnp.exp(group_sinks[:, None] - row_max)
        denominator = jnp.sum(weights, axis=2) + sink_weight
        probabilities = weights / denominator[:, :, None]
        sink_prob = sink_weight / denominator
        probs_low = probabilities.astype(jnp.bfloat16)
        outputs = jnp.einsum(
            "hij,jd->hid", probs_low, group_values, preferred_element_type=jnp.float32
        )
        row_delta = jnp.sum(outputs * jnp.swapaxes(grouped_d, 0, 1).astype(jnp.float32), axis=2)
        dot_grad = jnp.einsum(
            "ihd,jd->hij", grouped_d, group_values, preferred_element_type=jnp.float32
        )
        score_grad = (probabilities * (dot_grad - row_delta[:, :, None])).astype(jnp.bfloat16)
        query_parts.append(
            (
                jnp.einsum(
                    "hij,jd->ihd", score_grad, group_keys, preferred_element_type=jnp.float32
                )
                * score_scale
            ).reshape(tokens, group_size * HD)
        )
        key_parts.append(
            jnp.einsum("hij,ihd->jd", score_grad, grouped_q, preferred_element_type=jnp.float32)
            * score_scale
        )
        value_parts.append(
            jnp.einsum("hij,ihd->jd", probs_low, grouped_d, preferred_element_type=jnp.float32)
        )
        sink_parts.append(-jnp.sum(sink_prob * row_delta, axis=1))
    query_grad = jnp.concatenate(query_parts, axis=1).astype(jnp.bfloat16)
    return (
        query_grad,
        jnp.concatenate(key_parts, axis=1),
        jnp.concatenate(value_parts, axis=1),
        jnp.concatenate(sink_parts, axis=0),
    )


def shards(
    query_rows, key_rows, value_rows, output_grad, sink_logits, parent_branch, segment_length
):
    tail_len = WIN - 1
    own_queries = query_rows[0, 0, 0]
    own_keys = key_rows[0, 0, 0]
    own_values = value_rows[0, 0, 0]
    own_grad = output_grad[0, 0, 0]
    live_count = segment_length[0, 0, 0]
    parent = parent_branch[0, 0, 0]
    branch = lax.axis_index("expert")
    level = lax.axis_index("ctx")
    tail_start = live_count - tail_len
    own_tail = jnp.stack(
        [
            lax.dynamic_slice_in_dim(own_keys, tail_start, tail_len, 0),
            lax.dynamic_slice_in_dim(own_values, tail_start, tail_len, 0),
        ]
    )
    shifted = passed_along(own_tail, "ctx", 1)
    neighbours = padded(shifted[None], (("expert", 0),), 1)
    slot_index = parent - branch + 1
    parent_tail = lax.dynamic_index_in_dim(neighbours, slot_index, 0, keepdims=False)
    has_parent = level > 0
    query_grad, key_all, value_all, sink_terms = attend_backward(
        own_queries,
        own_keys,
        own_values,
        own_grad,
        parent_tail[0],
        parent_tail[1],
        live_count,
        has_parent,
        sink_logits,
    )
    tail_grads = jnp.stack([key_all[:tail_len], value_all[:tail_len]]).astype(jnp.bfloat16)
    slot_mask = (jnp.arange(3, dtype=jnp.int32) == slot_index) & has_parent
    slot_flags = slot_mask.astype(jnp.bfloat16)
    raised, raised_flags = passed_along((tail_grads, slot_flags), "ctx", -1)
    spread, spread_flags = (
        padded(raised[None], (("expert", 0),), 1),
        padded(raised_flags[None], (("expert", 0),), 1),
    )
    places = jnp.arange(3, dtype=jnp.int32)
    pick_table = (places[None, :] == (2 - places)[:, None]).astype(jnp.float32)
    weights = jnp.sum(spread_flags.astype(jnp.float32) * pick_table, axis=1)
    incoming = (
        weights[0] * spread[0].astype(jnp.float32)
        + weights[1] * spread[1].astype(jnp.float32)
        + weights[2] * spread[2].astype(jnp.float32)
    )
    own_rows = jnp.stack([key_all[tail_len:], value_all[tail_len:]])
    placed = lax.dynamic_update_slice_in_dim(jnp.zeros_like(own_rows), incoming, tail_start, 1)
    total_rows = (own_rows + placed).astype(jnp.bfloat16)
    sink_grad = summed_over(summed_over(sink_terms, ("dp", "ctx")), ("expert",))
    return (
        query_grad[None, None, None],
        total_rows[0][None, None, None],
        total_rows[1][None, None, None],
        sink_grad,
    )


def solution(mesh):
    return jax.shard_map(
        shards,
        mesh=mesh,
        in_specs=(
            P("dp", "ctx", "expert", None, None),
            P("dp", "ctx", "expert", None, None),
            P("dp", "ctx", "expert", None, None),
            P("dp", "ctx", "expert", None, None),
            P(),
            P("dp", "ctx", "expert"),
            P("dp", "ctx", "expert"),
        ),
        out_specs=(
            P("dp", "ctx", "expert", None, None),
            P("dp", "ctx", "expert", None, None),
            P("dp", "ctx", "expert", None, None),
            P(),
        ),
        check_vma=False,
    )
```

```python
import jax
import jax.numpy as jnp
from jax import lax
from jax.experimental import pallas as pl
from jax.experimental.pallas import tpu as pltpu
from jax.sharding import PartitionSpec as P

HQ = 32
HK = 4
HD = 64
WIN = 128
GROUP = HQ // HK
GCOLS = GROUP * HD
STEPS = 2
PER_STEP = HK // STEPS
LOW = -1e30
F32 = jnp.float32
BF16 = jnp.bfloat16

NT = (((1,), (1,)), ((), ()))
TN = (((0,), (0,)), ((), ()))
NN = (((1,), (0,)), ((), ()))


def mm(a, b, dims):
    return lax.dot_general(a, b, dims, preferred_element_type=F32)


def upper():
    c = lax.broadcasted_iota(jnp.int32, (WIN, WIN), 0)
    r = lax.broadcasted_iota(jnp.int32, (WIN, WIN), 1)
    return c > r


def one_head(s, dp, sink, alive):
    top = jnp.maximum(jnp.max(s, axis=0, keepdims=True), sink)
    e = jnp.exp(s - top)
    sink_e = jnp.exp(sink - top)
    inv = 1.0 / (jnp.sum(e, axis=0, keepdims=True) + sink_e)
    if alive is not None:
        inv = jnp.where(alive, inv, 0.0)
    p = e * inv
    low = p.astype(BF16)
    delta = jnp.sum(low.astype(F32) * dp, axis=0, keepdims=True)
    ds = (p * (dp - delta)).astype(BF16)
    return low, ds, sink_e * inv * delta


def forward_group(sub, keys, values, q, d, seen_upper, sinks, first, bias, alive, low, ds, sink_out, sink_base):
    for pair in range(GROUP // 2):
        at = pair * 2 * HD
        q2 = jnp.concatenate([q[:, at : at + HD], q[:, at + HD : at + 2 * HD]], axis=0)
        d2 = jnp.concatenate([d[:, at : at + HD], d[:, at + HD : at + 2 * HD]], axis=0)
        s2 = mm(keys, q2, NT)
        dp2 = mm(values, d2, NT)
        for one in range(2):
            h = pair * 2 + one
            lanes = slice(one * WIN, (one + 1) * WIN)
            s_up = s2[:WIN, lanes]
            if bias is not None:
                s_up = s_up + bias
            s = jnp.where(seen_upper, s_up, s2[WIN:, lanes])
            dp = jnp.where(seen_upper, dp2[:WIN, lanes], dp2[WIN:, lanes])
            l_h, ds_h, sink_h = one_head(s, dp, sinks[first + h], alive)
            cols = slice(h * WIN, (h + 1) * WIN)
            low[sub, :, cols] = l_h
            ds[sub, :, cols] = ds_h
            sink_out[pl.ds(sink_base + h, 1), :] = sink_h


def backward_group(keys, q, d, mask_up, low, ds):
    up8 = jnp.concatenate([mask_up] * GROUP, axis=1)
    low_up = low * up8
    ds_up = ds * up8
    low_all = jnp.concatenate([low_up, low - low_up], axis=0)
    ds_all = jnp.concatenate([ds_up, ds - ds_up], axis=0)
    q8 = jnp.concatenate([q[:, h * HD : (h + 1) * HD] for h in range(GROUP)], axis=0)
    d8 = jnp.concatenate([d[:, h * HD : (h + 1) * HD] for h in range(GROUP)], axis=0)
    dk = mm(ds_all, q8, NN) * (HD**-0.5)
    dv = mm(low_all, d8, NN)
    dqt = mm(keys, ds_all, TN).astype(BF16)
    parts = []
    for pair in range(GROUP // 2):
        at = pair * 2 * WIN
        two = jnp.concatenate([dqt[:, at : at + WIN], dqt[:, at + WIN : at + 2 * WIN]], axis=0)
        parts.append(two.T)
    return jnp.concatenate(parts, axis=1), dk, dv


def tail_kernel(length, k_ref, v_ref, out_ref):
    c = lax.broadcasted_iota(jnp.int32, (WIN, 2 * WIN), 0)
    j = lax.broadcasted_iota(jnp.int32, (WIN, 2 * WIN), 1)
    pick = jnp.where(j == c + (length[0] - WIN), 1.0, 0.0).astype(BF16)
    out_ref[:, : HK * HD] = mm(pick, k_ref[...], NN).astype(BF16)
    out_ref[:, HK * HD :] = mm(pick, v_ref[...], NN).astype(BF16)


def late_kernel(length, sinks, q_ref, d_ref, k_ref, v_ref, dq_ref, dk_ref, dv_ref, sink_ref, low, ds):
    step = pl.program_id(0)
    seen_upper = upper()
    mask_up = jnp.where(seen_upper, 1.0, 0.0).astype(BF16)
    alive = lax.broadcasted_iota(jnp.int32, (1, WIN), 1) < length[0] - WIN
    for sub in range(PER_STEP):
        cols = slice(sub * GCOLS, (sub + 1) * GCOLS)
        kv = slice(sub * HD, (sub + 1) * HD)
        keys = k_ref[:, kv] * (HD**-0.5)
        values = v_ref[:, kv]
        q = q_ref[:, cols]
        d = d_ref[:, cols]
        forward_group(sub, keys, values, q, d, seen_upper, sinks, (step * PER_STEP + sub) * GROUP, None, alive, low, ds, sink_ref, sub * GROUP)
        dq, dk, dv = backward_group(keys, q, d, mask_up, low[sub], ds[sub])
        dq_ref[:, cols] = dq
        dk_ref[:, kv] = dk
        dv_ref[:, kv] = dv


def early_kernel(place, sinks, q_ref, d_ref, k_ref, v_ref, ka, kb, kc, va, vb, vc, late_sink, low, ds, keys_out, sink_ref, sink_rows):
    step = pl.program_id(0)
    slot = place[0]
    bias = jnp.where(place[1] > 0, 0.0, LOW)
    seen_upper = upper()

    @pl.when(step == 0)
    def _():
        sink_rows[...] = jnp.zeros_like(sink_rows)

    def chosen(a, b, c):
        return jnp.where(slot == 0, a[...], jnp.where(slot == 1, b[...], c[...]))

    tail_k = chosen(ka, kb, kc)
    tail_v = chosen(va, vb, vc)
    for sub in range(PER_STEP):
        cols = slice(sub * GCOLS, (sub + 1) * GCOLS)
        kv = slice(sub * HD, (sub + 1) * HD)
        keys = jnp.concatenate([tail_k[:, kv], k_ref[:, kv]], axis=0) * (HD**-0.5)
        values = jnp.concatenate([tail_v[:, kv], v_ref[:, kv]], axis=0)
        keys_out[:, kv] = keys
        forward_group(sub, keys, values, q_ref[:, cols], d_ref[:, cols], seen_upper, sinks, (step * PER_STEP + sub) * GROUP, bias, None, low, ds, sink_rows, (step * PER_STEP + sub) * GROUP)

    @pl.when(step == STEPS - 1)
    def _():
        sink_rows[:HQ, :] = sink_rows[:HQ, :] + late_sink[...]
        total = -jnp.sum(sink_rows[...].T, axis=0, keepdims=True)
        sink_ref[...] = jnp.broadcast_to(total, sink_ref.shape)


def grads_kernel(place, q_ref, d_ref, keys_ref, low, ds, dq_in, dq_ref, tk_ref, tv_ref, ok_ref, ov_ref):
    del dq_in
    mask_up = jnp.where(upper(), 1.0, 0.0).astype(BF16)
    row = lax.broadcasted_iota(jnp.int32, (WIN, HD), 0)
    flag = (place[0] + 1).astype(F32)
    for sub in range(PER_STEP):
        cols = slice(sub * GCOLS, (sub + 1) * GCOLS)
        kv = slice(sub * HD, (sub + 1) * HD)
        dq, dk, dv = backward_group(keys_ref[:, kv], q_ref[:, cols], d_ref[:, cols], mask_up, low[sub], ds[sub])
        dq_ref[:, cols] = dq
        tk_ref[:, kv] = jnp.where(row == 0, flag, dk[:WIN]).astype(BF16)
        tv_ref[:, kv] = dv[:WIN].astype(BF16)
        ok_ref[:, kv] = dk[WIN:]
        ov_ref[:, kv] = dv[WIN:]


def final_kernel(length, dk_late, dv_late, ok, ov, ka, kb, kc, va, vb, vc, dk_ref, dv_ref):
    j = lax.broadcasted_iota(jnp.int32, (2 * WIN, WIN), 0)
    c = lax.broadcasted_iota(jnp.int32, (2 * WIN, WIN), 1)
    put = jnp.where((j == c + (length[0] - WIN)) & (c > 0), 1.0, 0.0).astype(BF16)
    dk = dk_late[...]
    dv = dv_late[...]
    for k_in, v_in, mark in ((ka, va, 3.0), (kb, vb, 2.0), (kc, vc, 1.0)):
        mine = jnp.max(k_in[:16, :WIN].astype(F32)[0:1, 0:1]) == mark
        picked = jnp.where(mine, put, jnp.zeros_like(put))
        dk = dk + mm(picked, k_in[...], NN)
        dv = dv + mm(picked, v_in[...], NN)
    half = slice(0, WIN)
    rest = slice(WIN, 2 * WIN)
    dk_ref[half, :] = (dk[half] + ok[...]).astype(BF16)
    dk_ref[rest, :] = dk[rest].astype(BF16)
    dv_ref[half, :] = (dv[half] + ov[...]).astype(BF16)
    dv_ref[rest, :] = dv[rest].astype(BF16)


SMEM = pl.BlockSpec(memory_space=pltpu.SMEM)
WHOLE = pl.BlockSpec(memory_space=pltpu.VMEM)
ANY = pl.BlockSpec(memory_space=pl.ANY)
PARAMS = pltpu.CompilerParams(vmem_limit_bytes=48 * 1024 * 1024)
KV = HK * HD
KV_STEP = KV // STEPS
COLS = HQ * HD
COLS_STEP = COLS // STEPS


def shaped(shape, dtype):
    return jax.ShapeDtypeStruct(shape, dtype)


def blocks(rows, cols, at):
    return pl.BlockSpec((rows, cols), lambda p: (at, p))


def cost(flops, size):
    return pl.CostEstimate(flops=flops, bytes_accessed=size, transcendentals=0)


def tails(length, k, v):
    return pl.pallas_call(
        tail_kernel,
        out_shape=shaped((WIN, 2 * KV), BF16),
        in_specs=[SMEM, WHOLE, WHOLE],
        out_specs=WHOLE,
        compiler_params=PARAMS,
        cost_estimate=cost(2 * 128 * 256 * 512, 400_000),
        name="tails",
    )(length, k, v)


def late_rows(length, sinks, q, d, k, v):
    return pl.pallas_call(
        late_kernel,
        grid=(STEPS,),
        out_shape=(
            shaped((2 * WIN, COLS), BF16),
            shaped((2 * WIN, KV), F32),
            shaped((2 * WIN, KV), F32),
            shaped((HQ, WIN), F32),
        ),
        in_specs=[
            SMEM,
            SMEM,
            blocks(WIN, COLS_STEP, 1),
            blocks(WIN, COLS_STEP, 1),
            blocks(2 * WIN, KV_STEP, 0),
            blocks(2 * WIN, KV_STEP, 0),
        ],
        out_specs=(
            blocks(WIN, COLS_STEP, 1),
            blocks(2 * WIN, KV_STEP, 0),
            blocks(2 * WIN, KV_STEP, 0),
            pl.BlockSpec((HQ // STEPS, WIN), lambda p: (p, 0)),
        ),
        scratch_shapes=[
            pltpu.VMEM((PER_STEP, WIN, GROUP * WIN), BF16),
            pltpu.VMEM((PER_STEP, WIN, GROUP * WIN), BF16),
        ],
        compiler_params=PARAMS,
        cost_estimate=cost(5 * 2 * 32 * 128 * 256 * 64 * 2, 2_500_000),
        name="late_rows",
    )(length, sinks, q, d, k, v)


def early_rows(place, sinks, q, d, k, v, lo, mid, hi, late_sink, copies):
    tail_k = blocks(WIN, KV_STEP, 0)
    tail_v = pl.BlockSpec((WIN, KV_STEP), lambda p: (0, STEPS + p))
    packed = pl.BlockSpec((PER_STEP, WIN, GROUP * WIN), lambda p: (p, 0, 0))
    return pl.pallas_call(
        early_kernel,
        grid=(STEPS,),
        out_shape=(
            shaped((HK, WIN, GROUP * WIN), BF16),
            shaped((HK, WIN, GROUP * WIN), BF16),
            shaped((2 * WIN, KV), BF16),
            shaped((copies, WIN), F32),
        ),
        in_specs=[
            SMEM,
            SMEM,
            blocks(WIN, COLS_STEP, 0),
            blocks(WIN, COLS_STEP, 0),
            blocks(WIN, KV_STEP, 0),
            blocks(WIN, KV_STEP, 0),
            tail_k,
            tail_k,
            tail_k,
            tail_v,
            tail_v,
            tail_v,
            pl.BlockSpec((HQ, WIN), lambda p: (0, 0)),
        ],
        out_specs=(packed, packed, blocks(2 * WIN, KV_STEP, 0), pl.BlockSpec((copies, WIN), lambda p: (0, 0))),
        scratch_shapes=[pltpu.VMEM((WIN, WIN), F32)],
        compiler_params=PARAMS,
        cost_estimate=cost(2 * 2 * 32 * 128 * 256 * 64 * 2, 2_500_000),
        name="early_rows",
    )(place, sinks, q, d, k, v, lo, mid, hi, lo, mid, hi, late_sink)


def early_grads(place, q, d, keys, low, ds, dq):
    packed = pl.BlockSpec((PER_STEP, WIN, GROUP * WIN), lambda p: (p, 0, 0))
    tail = blocks(WIN, KV_STEP, 0)
    return pl.pallas_call(
        grads_kernel,
        grid=(STEPS,),
        out_shape=(
            shaped((2 * WIN, COLS), BF16),
            shaped((WIN, KV), BF16),
            shaped((WIN, KV), BF16),
            shaped((WIN, KV), F32),
            shaped((WIN, KV), F32),
        ),
        in_specs=[
            SMEM,
            blocks(WIN, COLS_STEP, 0),
            blocks(WIN, COLS_STEP, 0),
            blocks(2 * WIN, KV_STEP, 0),
            packed,
            packed,
            ANY,
        ],
        out_specs=(blocks(WIN, COLS_STEP, 0), tail, tail, tail, tail),
        input_output_aliases={6: 0},
        compiler_params=PARAMS,
        cost_estimate=cost(3 * 2 * 32 * 128 * 256 * 64 * 2, 2_500_000),
        name="early_grads",
    )(place, q, d, keys, low, ds, dq)


def finish(length, dk_late, dv_late, ok, ov, lo, mid, hi):
    return pl.pallas_call(
        final_kernel,
        out_shape=(shaped((2 * WIN, KV), BF16), shaped((2 * WIN, KV), BF16)),
        in_specs=[SMEM] + [WHOLE] * 10,
        out_specs=(WHOLE, WHOLE),
        compiler_params=PARAMS,
        cost_estimate=cost(2 * 3 * 256 * 128 * 512, 2_000_000),
        name="finish",
    )(length, dk_late, dv_late, ok, ov, lo[0], mid[0], hi[0], lo[1], mid[1], hi[1])


def moved(rows, axis, by):
    count = lax.axis_size(axis)
    pairs = [(i, i + by) for i in range(count) if 0 <= i + by < count]
    return lax.ppermute(rows, axis, pairs)


def summed_over(copies, axes):
    return jnp.sum(lax.all_to_all(copies, axes, 0, 0, tiled=True), axis=0)


def shards(query_rows, key_rows, value_rows, output_grad, sink_logits, parent_branch, segment_length):
    q = query_rows[0, 0, 0]
    k = key_rows[0, 0, 0]
    v = value_rows[0, 0, 0]
    d = output_grad[0, 0, 0]
    length = segment_length.reshape(1)
    branch = lax.axis_index("expert")
    level = lax.axis_index("ctx")
    slot = parent_branch[0, 0, 0] - branch + 1
    place = jnp.stack([slot, (level > 0).astype(jnp.int32)]).astype(jnp.int32)

    own_tail = tails(length, k, v)
    mid = moved(own_tail, "ctx", 1)
    dq, dk_late, dv_late, late_sink = late_rows(length, sink_logits, q, d, k, v)
    lo = moved(mid, "expert", 1)
    hi = moved(mid, "expert", -1)
    plane = lax.axis_size("dp") * lax.axis_size("ctx")
    low, ds, keys, sink_copies = early_rows(place, sink_logits, q, d, k, v, lo, mid, hi, late_sink, plane)

    in_plane = summed_over(sink_copies, ("dp", "ctx"))
    dq, tail_k, tail_v, ok, ov = early_grads(place, q, d, keys, low, ds, dq)
    spread = jnp.broadcast_to(in_plane[None], (lax.axis_size("expert"),) + in_plane.shape)
    sink_grad = summed_over(spread, ("expert",))[:HQ]

    up = moved(jnp.stack([tail_k, tail_v]), "ctx", -1)
    up_lo = moved(up, "expert", 1)
    up_hi = moved(up, "expert", -1)
    dk, dv = finish(length, dk_late, dv_late, ok, ov, up_lo, up, up_hi)
    return dq[None, None, None], dk[None, None, None], dv[None, None, None], sink_grad


def solution(mesh):
    part = P("dp", "ctx", "expert", None, None)
    scalar = P("dp", "ctx", "expert")
    return jax.shard_map(
        shards,
        mesh=mesh,
        in_specs=(part, part, part, part, P(), scalar, scalar),
        out_specs=(part, part, part, P()),
        check_vma=False,
    )
```

```python
import functools

import jax
import jax.numpy as jnp
from jax import lax
from jax.experimental import pallas as pl
from jax.experimental.pallas import tpu as pltpu
from jax.sharding import PartitionSpec as P

HQ = 32
HK = 4
HD = 64
WIN = 128
GROUP = HQ // HK
GCOLS = GROUP * HD
PART = HK // 2
LOW = -1e30
F32 = jnp.float32
BF16 = jnp.bfloat16

NT = (((1,), (1,)), ((), ()))
TN = (((0,), (0,)), ((), ()))
NN = (((1,), (0,)), ((), ()))


def mm(a, b, dims):
    return lax.dot_general(a, b, dims, preferred_element_type=F32)


def upper():
    c = lax.broadcasted_iota(jnp.int32, (WIN, WIN), 0)
    r = lax.broadcasted_iota(jnp.int32, (WIN, WIN), 1)
    return c > r


def one_head(s, dp, sink, alive):
    top = jnp.maximum(jnp.max(s, axis=0, keepdims=True), sink)
    e = jnp.exp(s - top)
    sink_e = jnp.exp(sink - top)
    inv = 1.0 / (jnp.sum(e, axis=0, keepdims=True) + sink_e)
    if alive is not None:
        inv = jnp.where(alive, inv, 0.0)
    p = e * inv
    low = p.astype(BF16)
    delta = jnp.sum(low.astype(F32) * dp, axis=0, keepdims=True)
    ds = (p * (dp - delta)).astype(BF16)
    return low, ds, sink_e * inv * delta


def forward_group(sub, keys, values, q, d, seen_upper, sinks, first, bias, alive, low, ds, sink_out, sink_base):
    for pair in range(GROUP // 2):
        at = pair * 2 * HD
        q2 = jnp.concatenate([q[:, at : at + HD], q[:, at + HD : at + 2 * HD]], axis=0)
        d2 = jnp.concatenate([d[:, at : at + HD], d[:, at + HD : at + 2 * HD]], axis=0)
        s2 = mm(keys, q2, NT)
        dp2 = mm(values, d2, NT)
        for one in range(2):
            h = pair * 2 + one
            lanes = slice(one * WIN, (one + 1) * WIN)
            s_up = s2[:WIN, lanes]
            if bias is not None:
                s_up = s_up + bias
            s = jnp.where(seen_upper, s_up, s2[WIN:, lanes])
            dp = jnp.where(seen_upper, dp2[:WIN, lanes], dp2[WIN:, lanes])
            l_h, ds_h, sink_h = one_head(s, dp, sinks[first + h], alive)
            cols = slice(h * WIN, (h + 1) * WIN)
            low[sub, :, cols] = l_h
            ds[sub, :, cols] = ds_h
            sink_out[pl.ds(sink_base + h, 1), :] = sink_h


def stacked(rows):
    return jnp.concatenate([rows[:, h * HD : (h + 1) * HD] for h in range(GROUP)], axis=0)


def upper_mask():
    mask = jnp.where(upper(), 1.0, 0.0).astype(BF16)
    return jnp.concatenate([mask] * GROUP, axis=1)


def query_side(keys, ds_all):
    dqt = mm(keys, ds_all, TN).astype(BF16)
    parts = []
    for pair in range(GROUP // 2):
        at = pair * 2 * WIN
        two = jnp.concatenate([dqt[:, at : at + WIN], dqt[:, at + WIN : at + 2 * WIN]], axis=0)
        parts.append(two.T)
    return jnp.concatenate(parts, axis=1)


def one_hot(hit):
    return jnp.where(hit, 1.0, 0.0).astype(BF16)


def start_all(copies):
    for copy in copies:
        copy.start()


def carried(g, sources, targets, sems):
    copies = [pltpu.make_async_copy(src.at[g], dst.at[g], sems.at[2 * g + n]) for n, (src, dst) in enumerate(zip(sources, targets))]
    start_all(copies)
    return copies


def load_kernel(length, k_in, v_in, k_ref, v_ref, tail_ref, sems):
    copies = [pltpu.make_async_copy(src, dst, sems.at[n]) for n, (src, dst) in enumerate(((k_in, k_ref), (v_in, v_ref)))]
    start_all(copies)
    c = lax.broadcasted_iota(jnp.int32, (WIN, 2 * WIN), 0)
    j = lax.broadcasted_iota(jnp.int32, (WIN, 2 * WIN), 1)
    pick = one_hot(j == c + (length[0, 0, 0] - WIN))
    for copy, ref, part in zip(copies, (k_ref, v_ref), range(2)):
        copy.wait()
        tail_ref[part] = mm(pick, ref[...], NN).astype(BF16)


def late_kernel(length, sinks, k_ref, v_ref, q_in, d_in, q_ref, d_ref, low_out, ds_out, sink_ref, low, ds, sems, out_sems, *, first):
    copies = {}
    for at, rows in enumerate((slice(WIN, 2 * WIN), slice(0, WIN))):
        for g in range(PART):
            for n, (src, dst) in enumerate(((q_in, q_ref), (d_in, d_ref))):
                here = slice(g * GCOLS, (g + 1) * GCOLS)
                there = slice((first + g) * GCOLS, (first + g + 1) * GCOLS)
                copies[at, g, n] = pltpu.make_async_copy(src.at[rows, there], dst.at[rows, here], sems.at[(at * PART + g) * 2 + n])
                copies[at, g, n].start()
    seen_upper = upper()
    alive = lax.broadcasted_iota(jnp.int32, (1, WIN), 1) < length[0, 0, 0] - WIN
    written = []
    for g in range(PART):
        copies[0, g, 0].wait()
        copies[0, g, 1].wait()
        cols = slice(g * GCOLS, (g + 1) * GCOLS)
        kv = slice((first + g) * HD, (first + g + 1) * HD)
        keys = k_ref[:, kv] * (HD**-0.5)
        forward_group(g, keys, v_ref[:, kv], q_ref[WIN:, cols], d_ref[WIN:, cols], seen_upper, sinks, (first + g) * GROUP, None, alive, low, ds, sink_ref, g * GROUP)
        written += carried(g, (low, ds), (low_out, ds_out), out_sems)
    for g in range(PART):
        copies[1, g, 0].wait()
        copies[1, g, 1].wait()
    for copy in written:
        copy.wait()


def early_kernel(parent, branch, level, sinks, qa, qb, da, db, k_ref, v_ref, lo, mid, hi, late_a, late_b, low_out, ds_out, keys_ref, sink_ref, sink_rows, low, ds, out_sems):
    slot = parent[0, 0, 0] - branch[0] + 1
    bias = jnp.where(level[0] > 0, 0.0, LOW)
    seen_upper = upper()
    sink_rows[HQ:, :] = jnp.zeros((WIN - HQ, WIN), F32)
    written = []
    tail = jnp.where(slot == 0, lo[...], jnp.where(slot == 1, mid[...], hi[...]))
    for g in range(HK):
        q_ref, d_ref = ((qa, da), (qb, db))[g // PART]
        cols = slice(g % PART * GCOLS, (g % PART + 1) * GCOLS)
        kv = slice(g * HD, (g + 1) * HD)
        keys = jnp.concatenate([tail[0, :, kv], k_ref[:WIN, kv]], axis=0) * (HD**-0.5)
        values = jnp.concatenate([tail[1, :, kv], v_ref[:WIN, kv]], axis=0)
        keys_ref[:, kv] = keys
        forward_group(g, keys, values, q_ref[:WIN, cols], d_ref[:WIN, cols], seen_upper, sinks, g * GROUP, bias, None, low, ds, sink_rows, g * GROUP)
        written += carried(g, (low, ds), (low_out, ds_out), out_sems)
    half = HQ // 2
    sink_rows[:half, :] = sink_rows[:half, :] + late_a[...]
    sink_rows[half:HQ, :] = sink_rows[half:HQ, :] + late_b[...]
    total = -jnp.sum(sink_rows[...].T, axis=0, keepdims=True)
    sink_ref[...] = jnp.broadcast_to(total, sink_ref.shape)
    for copy in written:
        copy.wait()


def backward_group(g, q_ref, d_ref, cols, rows, low, ds, mask):
    ds_up = ds * mask
    ds_down = ds - ds_up
    low_up = low * mask
    low_down = low - low_up
    q8 = stacked(q_ref[rows, cols])
    d8 = stacked(d_ref[rows, cols])
    ds_all = jnp.concatenate([ds_up, ds_down], axis=0)
    low_all = jnp.concatenate([low_up, low_down], axis=0)
    return ds_all, mm(ds_all, q8, NN) * (HD**-0.5), mm(low_all, d8, NN)


def early_grads_kernel(parent, branch, qa, qb, da, db, keys_ref, low_in, ds_in, dq_out, own_ref, tail_ref, dq_ref, low, ds, sems, in_sems):
    came = [carried(g, (low_in, ds_in), (low, ds), in_sems) for g in range(HK)]
    mask = upper_mask()
    flag = (parent[0, 0, 0] - branch[0] + 2).astype(F32)
    row = lax.broadcasted_iota(jnp.int32, (WIN, HD), 0)
    rows = slice(0, WIN)
    copies = []
    for g in range(HK):
        q_ref, d_ref = ((qa, da), (qb, db))[g // PART]
        cols = slice(g % PART * GCOLS, (g % PART + 1) * GCOLS)
        kv = slice(g * HD, (g + 1) * HD)
        for copy in came[g]:
            copy.wait()
        ds_all, dk, dv = backward_group(g, q_ref, d_ref, cols, rows, low[g], ds[g], mask)
        tail_ref[0, :, kv] = jnp.where(row == 0, flag, dk[:WIN]).astype(BF16)
        tail_ref[1, :, kv] = dv[:WIN].astype(BF16)
        own_ref[0, :, kv] = dk[WIN:]
        own_ref[1, :, kv] = dv[WIN:]
        out = slice(g * GCOLS, (g + 1) * GCOLS)
        dq_ref[:, out] = query_side(keys_ref[:, kv], ds_all)
        copies.append(pltpu.make_async_copy(dq_ref.at[:, out], dq_out.at[rows, out], sems.at[g]))
        copies[-1].start()
    for copy in copies:
        copy.wait()


def late_grads_kernel(qa, qb, da, db, k_ref, low_a, low_b, ds_a, ds_b, dq_in, dq_out, own_ref, dq_ref, low, ds, sems, in_sems):
    del dq_in
    came = []
    for g in range(HK):
        low_in, ds_in = ((low_a, ds_a), (low_b, ds_b))[g // PART]
        for n, (src, dst) in enumerate(((low_in, low), (ds_in, ds))):
            came.append(pltpu.make_async_copy(src.at[g % PART], dst.at[g], in_sems.at[2 * g + n]))
    start_all(came)
    mask = upper_mask()
    rows = slice(WIN, 2 * WIN)
    copies = []
    for g in range(HK):
        q_ref, d_ref = ((qa, da), (qb, db))[g // PART]
        cols = slice(g % PART * GCOLS, (g % PART + 1) * GCOLS)
        kv = slice(g * HD, (g + 1) * HD)
        came[2 * g].wait()
        came[2 * g + 1].wait()
        ds_all, own_ref[0, :, kv], own_ref[1, :, kv] = backward_group(g, q_ref, d_ref, cols, rows, low[g], ds[g], mask)
        out = slice(g * GCOLS, (g + 1) * GCOLS)
        dq_ref[:, out] = query_side(k_ref[:, kv] * (HD**-0.5), ds_all)
        copies.append(pltpu.make_async_copy(dq_ref.at[:, out], dq_out.at[rows, out], sems.at[g]))
        copies[-1].start()
    for copy in copies:
        copy.wait()


def finish_kernel(length, own, early_own, lo, mid, hi, dk_ref, dv_ref):
    j = lax.broadcasted_iota(jnp.int32, (2 * WIN, WIN), 0)
    c = lax.broadcasted_iota(jnp.int32, (2 * WIN, WIN), 1)
    put = (j == c + (length[0, 0, 0] - WIN)) & (c > 0)
    picked = []
    for child, mark in ((lo, 3.0), (mid, 2.0), (hi, 1.0)):
        mine = jnp.max(child[0, :16, :WIN].astype(F32)[0:1, 0:1]) == mark
        picked.append(one_hot(put & mine))
    pick = jnp.concatenate(picked, axis=1)
    for part, out in enumerate((dk_ref, dv_ref)):
        children = jnp.concatenate([lo[part], mid[part], hi[part]], axis=0)
        total = own[part] + mm(pick, children, NN)
        out[:WIN, :] = (total[:WIN] + early_own[part]).astype(BF16)
        out[WIN:, :] = total[WIN:].astype(BF16)


def add_up_kernel(rows, out):
    out[...] = jnp.broadcast_to(jnp.sum(rows[...], axis=0, keepdims=True), out.shape)


SMEM = pl.BlockSpec(memory_space=pltpu.SMEM)
VMEM = pl.BlockSpec(memory_space=pltpu.VMEM)
RESULT = pl.BlockSpec(memory_space=pltpu.VMEM)
HBM = pl.BlockSpec(memory_space=pltpu.HBM)
PARAMS = pltpu.CompilerParams(vmem_limit_bytes=40 * 1024 * 1024)
KV = HK * HD
COLS = HQ * HD
DMA = pltpu.SemaphoreType.DMA
PACKED = (HK, WIN, GROUP * WIN)
PACKED_PART = (PART, WIN, GROUP * WIN)


def shaped(shape, dtype):
    return jax.ShapeDtypeStruct(shape, dtype)


def cost(products, size):
    return pl.CostEstimate(flops=products * 2 * 32 * 128 * 256 * 64, bytes_accessed=size, transcendentals=0)


SMALL = pl.CostEstimate(flops=1000, bytes_accessed=1000, transcendentals=0)


def held(operand, spec):
    space = {id(VMEM): pltpu.VMEM, id(HBM): pltpu.HBM}.get(id(spec), pl.ANY)
    return pltpu.with_memory_space_constraint(operand, space)


def made(spec, shape, dtype):
    space = {id(VMEM): pltpu.VMEM, id(HBM): pltpu.HBM}.get(id(spec), shaped)
    return space(shape, dtype)


def call(kernel, name, ins, outs, scratch, estimate, *operands, aliases=None):
    operands = [held(operand, spec) for operand, spec in zip(operands, ins)]
    return pl.pallas_call(
        kernel,
        in_specs=ins,
        out_specs=tuple(spec for spec, _, _ in outs),
        out_shape=tuple(made(*out) for out in outs),
        scratch_shapes=scratch,
        compiler_params=PARAMS,
        input_output_aliases=aliases or {},
        cost_estimate=estimate,
        name=name,
    )(*operands)


def load(length, k, v):
    return call(
        load_kernel,
        "load",
        [SMEM, HBM, HBM],
        [(VMEM, (2 * WIN, KV), BF16), (VMEM, (2 * WIN, KV), BF16), (VMEM, (2, WIN, KV), BF16)],
        [DMA((2,))],
        cost(1, 400_000),
        length, k, v,
    )


def late_rows(length, sinks, k, v, q, d, first):
    return call(
        functools.partial(late_kernel, first=first),
        "late_rows",
        [SMEM, SMEM, VMEM, VMEM, HBM, HBM],
        [
            (VMEM, (2 * WIN, COLS // 2), BF16),
            (VMEM, (2 * WIN, COLS // 2), BF16),
            (HBM, PACKED_PART, BF16),
            (HBM, PACKED_PART, BF16),
            (VMEM, (HQ // 2, WIN), F32),
        ],
        [pltpu.VMEM(PACKED_PART, BF16), pltpu.VMEM(PACKED_PART, BF16), DMA((4 * PART,)), DMA((2 * PART,))],
        cost(4, 2_500_000),
        length, sinks, k, v, q, d,
    )


def early_rows(parent, branch, level, sinks, qa, qb, da, db, k, v, lo, mid, hi, late_a, late_b, copies):
    return call(
        early_kernel,
        "early_rows",
        [SMEM] * 4 + [VMEM] * 11,
        [
            (HBM, PACKED, BF16),
            (HBM, PACKED, BF16),
            (VMEM, (2 * WIN, KV), BF16),
            (RESULT, (copies, WIN), F32),
        ],
        [pltpu.VMEM((WIN, WIN), F32), pltpu.VMEM(PACKED, BF16), pltpu.VMEM(PACKED, BF16), DMA((2 * HK,))],
        cost(4, 5_000_000),
        parent, branch, level, sinks, qa, qb, da, db, k, v, lo, mid, hi, late_a, late_b,
    )


def early_grads(parent, branch, qa, qb, da, db, keys, low, ds):
    return call(
        early_grads_kernel,
        "early_grads",
        [SMEM] * 2 + [VMEM] * 5 + [HBM] * 2,
        [(HBM, (2 * WIN, COLS), BF16), (VMEM, (2, WIN, KV), F32), (VMEM, (2, WIN, KV), BF16)],
        [pltpu.VMEM((WIN, COLS), BF16), pltpu.VMEM(PACKED, BF16), pltpu.VMEM(PACKED, BF16), DMA((HK,)), DMA((2 * HK,))],
        SMALL,
        parent, branch, qa, qb, da, db, keys, low, ds,
    )


def late_grads(qa, qb, da, db, k, low_a, low_b, ds_a, ds_b, dq):
    return call(
        late_grads_kernel,
        "late_grads",
        [VMEM] * 5 + [HBM] * 5,
        [(HBM, (2 * WIN, COLS), BF16), (VMEM, (2, 2 * WIN, KV), F32)],
        [pltpu.VMEM((WIN, COLS), BF16), pltpu.VMEM(PACKED, BF16), pltpu.VMEM(PACKED, BF16), DMA((HK,)), DMA((2 * HK,))],
        SMALL,
        qa, qb, da, db, k, low_a, low_b, ds_a, ds_b, dq,
        aliases={9: 0},
    )


def finish(length, own, early_own, lo, mid, hi):
    return call(
        finish_kernel,
        "finish",
        [SMEM] + [VMEM] * 5,
        [(RESULT, (2 * WIN, KV), BF16), (RESULT, (2 * WIN, KV), BF16)],
        [],
        SMALL,
        length, own, early_own, lo, mid, hi,
    )


def add_up(rows, copies):
    return call(add_up_kernel, "add_up", [VMEM], [(VMEM, (copies, WIN), F32)], [], cost(100, 100), rows)[0]


def moved(rows, axis, by):
    count = lax.axis_size(axis)
    pairs = [(i, i + by) for i in range(count) if 0 <= i + by < count]
    return lax.ppermute(rows, axis, pairs)


def raised(rows, by):
    levels, branches = lax.axis_size("ctx"), lax.axis_size("expert")
    pairs = [
        (level * branches + b, (level - 1) * branches + b + by)
        for level in range(1, levels)
        for b in range(branches)
        if 0 <= b + by < branches
    ]
    return lax.ppermute(rows, ("ctx", "expert"), pairs)


def shards(query_rows, key_rows, value_rows, output_grad, sink_logits, parent_branch, segment_length):
    q = query_rows[0, 0, 0]
    k = key_rows[0, 0, 0]
    v = value_rows[0, 0, 0]
    d = output_grad[0, 0, 0]
    branch = lax.axis_index("expert").astype(jnp.int32).reshape(1)
    level = lax.axis_index("ctx").astype(jnp.int32).reshape(1)
    plane = lax.axis_size("dp") * lax.axis_size("ctx")
    experts = lax.axis_size("expert")

    k, v, own_tail = load(segment_length, k, v)
    mid = moved(own_tail, "ctx", 1)
    qa, da, low_a, ds_a, late_a = late_rows(segment_length, sink_logits, k, v, q, d, 0)
    mid, late_a, parent = lax.optimization_barrier((mid, late_a, parent_branch))
    lo = moved(mid, "expert", 1)
    hi = moved(mid, "expert", -1)
    qb, db, low_b, ds_b, late_b = late_rows(segment_length, sink_logits, k, v, q, d, PART)
    low, ds, keys, sinks = early_rows(parent, branch, level, sink_logits, qa, qb, da, db, k, v, lo, mid, hi, late_a, late_b, experts)

    column = lax.all_to_all(sinks, "expert", 0, 0, tiled=True)
    dq, early_own, tail = early_grads(parent, branch, qa, qb, da, db, keys, low, ds)
    up = raised(tail, 0)
    dq, own = late_grads(qa, qb, da, db, k, low_a, low_b, ds_a, ds_b, dq)
    up_lo = raised(tail, 1)
    up_hi = raised(tail, -1)
    everywhere = lax.all_to_all(add_up(column, plane), ("dp", "ctx"), 0, 0, tiled=True)
    dk, dv = finish(segment_length, own, early_own, up_lo, up, up_hi)
    everywhere, dk = lax.optimization_barrier((everywhere, dk))
    sink_grad = jnp.sum(everywhere, axis=0)[:HQ]
    return dq[None, None, None], dk[None, None, None], dv[None, None, None], sink_grad


def solution(mesh):
    part = P("dp", "ctx", "expert", None, None)
    scalar = P("dp", "ctx", "expert")
    return jax.shard_map(
        shards,
        mesh=mesh,
        in_specs=(part, part, part, part, P(), scalar, scalar),
        out_specs=(part, part, part, P()),
        check_vma=False,
    )
```

```python
import functools

import jax
import jax.numpy as jnp
from jax import lax
from jax.experimental import pallas as pl
from jax.experimental.pallas import tpu as pltpu
from jax.sharding import PartitionSpec as P

HQ = 32
HK = 4
HD = 64
WIN = 128
GROUP = HQ // HK
GCOLS = GROUP * HD
LOW = -1e30
F32 = jnp.float32
BF16 = jnp.bfloat16

NT = (((1,), (1,)), ((), ()))
TN = (((0,), (0,)), ((), ()))
NN = (((1,), (0,)), ((), ()))


def mm(a, b, dims):
    return lax.dot_general(a, b, dims, preferred_element_type=F32)


def upper():
    c = lax.broadcasted_iota(jnp.int32, (WIN, WIN), 0)
    r = lax.broadcasted_iota(jnp.int32, (WIN, WIN), 1)
    return c > r


def one_head(s, dp, sink, alive):
    top = jnp.maximum(jnp.max(s, axis=0, keepdims=True), sink)
    e = jnp.exp(s - top)
    sink_e = jnp.exp(sink - top)
    inv = 1.0 / (jnp.sum(e, axis=0, keepdims=True) + sink_e)
    if alive is not None:
        inv = jnp.where(alive, inv, 0.0)
    p = e * inv
    low = p.astype(BF16)
    delta = jnp.sum(low.astype(F32) * dp, axis=0, keepdims=True)
    ds = (p * (dp - delta)).astype(BF16)
    return low, ds, sink_e * inv * delta


def forward_group(sub, keys, values, q, d, seen_upper, sinks, first, bias, alive, low, ds, sink_out, sink_base):
    for pair in range(GROUP // 2):
        at = pair * 2 * HD
        q2 = jnp.concatenate([q[:, at : at + HD], q[:, at + HD : at + 2 * HD]], axis=0)
        d2 = jnp.concatenate([d[:, at : at + HD], d[:, at + HD : at + 2 * HD]], axis=0)
        s2 = mm(keys, q2, NT)
        dp2 = mm(values, d2, NT)
        for one in range(2):
            h = pair * 2 + one
            lanes = slice(one * WIN, (one + 1) * WIN)
            s_up = s2[:WIN, lanes]
            if bias is not None:
                s_up = s_up + bias
            s = jnp.where(seen_upper, s_up, s2[WIN:, lanes])
            dp = jnp.where(seen_upper, dp2[:WIN, lanes], dp2[WIN:, lanes])
            l_h, ds_h, sink_h = one_head(s, dp, sinks[first + h], alive)
            cols = slice(h * WIN, (h + 1) * WIN)
            low[sub, :, cols] = l_h
            ds[sub, :, cols] = ds_h
            sink_out[pl.ds(sink_base + h, 1), :] = sink_h


def stacked(rows):
    return jnp.concatenate([rows[:, h * HD : (h + 1) * HD] for h in range(GROUP)], axis=0)


def upper_mask():
    mask = jnp.where(upper(), 1.0, 0.0).astype(BF16)
    return jnp.concatenate([mask] * GROUP, axis=1)


def query_side(keys, ds_all):
    dqt = mm(keys, ds_all, TN).astype(BF16)
    parts = []
    for pair in range(GROUP // 2):
        at = pair * 2 * WIN
        two = jnp.concatenate([dqt[:, at : at + WIN], dqt[:, at + WIN : at + 2 * WIN]], axis=0)
        parts.append(two.T)
    return jnp.concatenate(parts, axis=1)


def one_hot(hit):
    return jnp.where(hit, 1.0, 0.0).astype(BF16)


def start_all(copies):
    for copy in copies:
        copy.start()


def carried(g, sources, targets, sems):
    copies = [pltpu.make_async_copy(src.at[g], dst.at[g], sems.at[2 * g + n]) for n, (src, dst) in enumerate(zip(sources, targets))]
    start_all(copies)
    return copies


def columns_of(g, first, sources, targets, sems):
    cols = slice(g * GCOLS, (g + 1) * GCOLS)
    copies = [
        pltpu.make_async_copy(src.at[pl.ds(first, WIN), cols], dst.at[:, cols], sems.at[2 * g + n])
        for n, (src, dst) in enumerate(zip(sources, targets))
    ]
    start_all(copies)
    return copies


def load_kernel(length, k_in, v_in, q_in, d_in, k_ref, v_ref, tail_ref, q_first, d_first, sems, first_sems):
    copies = [pltpu.make_async_copy(src, dst, sems.at[n]) for n, (src, dst) in enumerate(((k_in, k_ref), (v_in, v_ref)))]
    start_all(copies)
    firsts = columns_of(0, WIN, (q_in, d_in), (q_first, d_first), first_sems)
    c = lax.broadcasted_iota(jnp.int32, (WIN, 2 * WIN), 0)
    j = lax.broadcasted_iota(jnp.int32, (WIN, 2 * WIN), 1)
    pick = one_hot(j == c + (length[0, 0, 0] - WIN))
    for copy, ref, part in zip(copies, (k_ref, v_ref), range(2)):
        copy.wait()
        tail_ref[part] = mm(pick, ref[...], NN).astype(BF16)
    for copy in firsts:
        copy.wait()


def late_kernel(length, sinks_in, k_ref, v_ref, q_first, d_first, q_in, d_in, q_early, d_early, q_last, d_last, low_out, ds_out, low_last, ds_last, sink_ref, q_ref, d_ref, low, ds, sinks, sems, early_sems, out_sems, sink_sem):
    sinks_copy = pltpu.make_async_copy(sinks_in, sinks, sink_sem)
    sinks_copy.start()
    came = {g: columns_of(g, WIN, (q_in, d_in), (q_ref, d_ref), sems) for g in range(1, LAST)}
    cols = slice(LAST * GCOLS, HK * GCOLS)
    came[LAST] = [
        pltpu.make_async_copy(src.at[pl.ds(WIN, WIN), cols], dst, sems.at[2 * LAST + n])
        for n, (src, dst) in enumerate(((q_in, q_last), (d_in, d_last)))
    ]
    brought = [
        pltpu.make_async_copy(src.at[pl.ds(0, WIN), :], dst, early_sems.at[n])
        for n, (src, dst) in enumerate(((q_in, q_early), (d_in, d_early)))
    ]
    start_all(came[LAST] + brought)
    seen_upper = upper()
    alive = lax.broadcasted_iota(jnp.int32, (1, WIN), 1) < length[0, 0, 0] - WIN
    written = []
    sinks_copy.wait()
    for g in range(HK):
        cols = slice(g * GCOLS, (g + 1) * GCOLS)
        kv = slice(g * HD, (g + 1) * HD)
        for copy in came.get(g, ()):
            copy.wait()
        if g == 0:
            q, d = q_first[...], d_first[...]
        elif g < LAST:
            q, d = q_ref[:, cols], d_ref[:, cols]
        else:
            q, d = q_last[...], d_last[...]
        to = (g, low, ds) if g < LAST else (0, low_last, ds_last)
        keys = k_ref[:, kv] * (HD**-0.5)
        forward_group(to[0], keys, v_ref[:, kv], q, d, seen_upper, sinks, g * GROUP, None, alive, to[1], to[2], sink_ref, g * GROUP)
        if g < LAST:
            written += carried(g, (low, ds), (low_out, ds_out), out_sems)
    for copy in brought + written:
        copy.wait()


def early_kernel(parent, branch, level, sinks_in, q_ref, d_ref, k_ref, v_ref, lo, mid, hi, late_sink, low_out, ds_out, low_last, ds_last, keys_ref, sink_ref, sink_rows, low, ds, sinks, out_sems, sink_sem):
    sinks_copy = pltpu.make_async_copy(sinks_in, sinks, sink_sem)
    sinks_copy.start()
    slot = parent[0, 0, 0] - branch[0] + 1
    bias = jnp.where(level[0] > 0, 0.0, LOW)
    seen_upper = upper()
    sink_rows[HQ:, :] = jnp.zeros((WIN - HQ, WIN), F32)
    written = []
    tail = jnp.where(slot == 0, lo[...], jnp.where(slot == 1, mid[...], hi[...]))
    sinks_copy.wait()
    for g in range(HK):
        cols = slice(g * GCOLS, (g + 1) * GCOLS)
        kv = slice(g * HD, (g + 1) * HD)
        keys = jnp.concatenate([tail[0, :, kv], k_ref[:WIN, kv]], axis=0) * (HD**-0.5)
        values = jnp.concatenate([tail[1, :, kv], v_ref[:WIN, kv]], axis=0)
        keys_ref[:, kv] = keys
        to = (g, low, ds) if g < LAST else (0, low_last, ds_last)
        forward_group(to[0], keys, values, q_ref[:, cols], d_ref[:, cols], seen_upper, sinks, g * GROUP, bias, None, to[1], to[2], sink_rows, g * GROUP)
        if g < LAST:
            written += carried(g, (low, ds), (low_out, ds_out), out_sems)
    sink_rows[:HQ, :] = sink_rows[:HQ, :] + late_sink[...]
    total = -jnp.sum(sink_rows[...].T, axis=0, keepdims=True)
    sink_ref[...] = jnp.broadcast_to(total, sink_ref.shape)
    for copy in written:
        copy.wait()


def one_side(keys, q, d, low, ds, mask):
    ds_up = ds * mask
    low_up = low * mask
    ds_all = jnp.concatenate([ds_up, ds - ds_up], axis=0)
    low_all = jnp.concatenate([low_up, low - low_up], axis=0)
    dk = mm(ds_all, stacked(q), NN) * (HD**-0.5)
    dv = mm(low_all, stacked(d), NN)
    return query_side(keys, ds_all), dk, dv


def early_grads_kernel(parent, branch, q_ref, d_ref, keys_ref, low_last, ds_last, low_in, ds_in, dq_out, own_ref, tail_ref, dq_ref, low, ds, sems, in_sems):
    came = [carried(g, (low_in, ds_in), (low, ds), in_sems) for g in range(LAST)]
    mask = upper_mask()
    flag = (parent[0, 0, 0] - branch[0] + 2).astype(F32)
    row = lax.broadcasted_iota(jnp.int32, (WIN, HD), 0)
    rows = slice(0, WIN)
    copies = []
    for g in (LAST,) + tuple(range(LAST)):
        cols = slice(g * GCOLS, (g + 1) * GCOLS)
        kv = slice(g * HD, (g + 1) * HD)
        if g < LAST:
            for copy in came[g]:
                copy.wait()
        low_g, ds_g = (low[g], ds[g]) if g < LAST else (low_last[0], ds_last[0])
        dq_ref[:, cols], dk, dv = one_side(keys_ref[:, kv], q_ref[:, cols], d_ref[:, cols], low_g, ds_g, mask)
        copies.append(pltpu.make_async_copy(dq_ref.at[:, cols], dq_out.at[rows, cols], sems.at[g]))
        copies[-1].start()
        tail_ref[0, :, kv] = jnp.where(row == 0, flag, dk[:WIN]).astype(BF16)
        tail_ref[1, :, kv] = dv[:WIN].astype(BF16)
        own_ref[0, :, kv] = dk[WIN:]
        own_ref[1, :, kv] = dv[WIN:]
    for copy in copies:
        copy.wait()


def late_grads_kernel(length, q_last, d_last, k_ref, own, lo, mid, hi, low_last, ds_last, q_in, d_in, low_in, ds_in, dq_in, dq_out, dk_ref, dv_ref, dq_ref, q_ref, d_ref, low, ds, sems, in_sems, q_sems):
    del dq_in
    came = []
    for g in range(LAST):
        came.append(carried(g, (low_in, ds_in), (low, ds), in_sems) + columns_of(g, WIN, (q_in, d_in), (q_ref, d_ref), q_sems))
    mask = upper_mask()
    j = lax.broadcasted_iota(jnp.int32, (2 * WIN, WIN), 0)
    c = lax.broadcasted_iota(jnp.int32, (2 * WIN, WIN), 1)
    put = (j == c + (length[0, 0, 0] - WIN)) & (c > 0)
    picked = []
    for child, mark in ((lo, 3.0), (mid, 2.0), (hi, 1.0)):
        mine = jnp.max(child[0, :16, :WIN].astype(F32)[0:1, 0:1]) == mark
        picked.append(one_hot(put & mine))
    pick = jnp.concatenate(picked, axis=1)
    sums = []
    for part in range(2):
        children = jnp.concatenate([lo[part], mid[part], hi[part]], axis=0)
        sums.append(mm(pick, children, NN))
    rows = slice(WIN, 2 * WIN)
    copies = []
    for g in (LAST,) + tuple(range(LAST)):
        cols = slice(g * GCOLS, (g + 1) * GCOLS)
        kv = slice(g * HD, (g + 1) * HD)
        if g < LAST:
            for copy in came[g]:
                copy.wait()
        if g < LAST:
            q_g, d_g, low_g, ds_g = q_ref[:, cols], d_ref[:, cols], low[g], ds[g]
        else:
            q_g, d_g, low_g, ds_g = q_last[...], d_last[...], low_last[0], ds_last[0]
        dq_ref[:, cols], dk, dv = one_side(k_ref[:, kv] * (HD**-0.5), q_g, d_g, low_g, ds_g, mask)
        copies.append(pltpu.make_async_copy(dq_ref.at[:, cols], dq_out.at[rows, cols], sems.at[g]))
        copies[-1].start()
        for part, (late, out) in enumerate(((dk, dk_ref), (dv, dv_ref))):
            total = late + sums[part][:, kv]
            out[:WIN, kv] = (total[:WIN] + own[part, :, kv]).astype(BF16)
            out[WIN:, kv] = total[WIN:].astype(BF16)
    for copy in copies:
        copy.wait()


def add_up_kernel(rows, out):
    out[...] = jnp.broadcast_to(jnp.sum(rows[...], axis=0, keepdims=True), out.shape)


SMEM = pl.BlockSpec(memory_space=pltpu.SMEM)
VMEM = pl.BlockSpec(memory_space=pltpu.VMEM)
RESULT = pl.BlockSpec(memory_space=pltpu.VMEM)
HBM = pl.BlockSpec(memory_space=pltpu.HBM)
PARAMS = pltpu.CompilerParams(vmem_limit_bytes=40 * 1024 * 1024)
KV = HK * HD
COLS = HQ * HD
DMA = pltpu.SemaphoreType.DMA
LAST = HK - 1
PACKED = (LAST, WIN, GROUP * WIN)
PACKED_LAST = (1, WIN, GROUP * WIN)


def shaped(shape, dtype):
    return jax.ShapeDtypeStruct(shape, dtype)


def cost(products, size):
    return pl.CostEstimate(flops=products * 2 * 32 * 128 * 256 * 64, bytes_accessed=size, transcendentals=0)


SMALL = pl.CostEstimate(flops=1000, bytes_accessed=1000, transcendentals=0)


def held(operand, spec):
    space = {id(VMEM): pltpu.VMEM, id(HBM): pltpu.HBM}.get(id(spec), pl.ANY)
    return pltpu.with_memory_space_constraint(operand, space)


def made(spec, shape, dtype):
    space = {id(VMEM): pltpu.VMEM, id(HBM): pltpu.HBM}.get(id(spec), shaped)
    return space(shape, dtype)


def call(kernel, name, ins, outs, scratch, estimate, *operands, aliases=None):
    operands = [held(operand, spec) for operand, spec in zip(operands, ins)]
    return pl.pallas_call(
        kernel,
        in_specs=ins,
        out_specs=tuple(spec for spec, _, _ in outs),
        out_shape=tuple(made(*out) for out in outs),
        scratch_shapes=scratch,
        compiler_params=PARAMS,
        input_output_aliases=aliases or {},
        cost_estimate=estimate,
        name=name,
    )(*operands)


def load(length, k, v, q, d):
    return call(
        load_kernel,
        "load",
        [SMEM] + [HBM] * 4,
        [
            (VMEM, (2 * WIN, KV), BF16),
            (VMEM, (2 * WIN, KV), BF16),
            (VMEM, (2, WIN, KV), BF16),
            (VMEM, (WIN, GCOLS), BF16),
            (VMEM, (WIN, GCOLS), BF16),
        ],
        [DMA((2,)), DMA((2,))],
        cost(1, 400_000),
        length, k, v, q, d,
    )


def late_rows(length, sinks, k, v, q_first, d_first, q, d):
    return call(
        late_kernel,
        "late_rows",
        [SMEM, HBM] + [VMEM] * 4 + [HBM] * 2,
        [
            (VMEM, (WIN, COLS), BF16),
            (VMEM, (WIN, COLS), BF16),
            (VMEM, (WIN, GCOLS), BF16),
            (VMEM, (WIN, GCOLS), BF16),
            (HBM, PACKED, BF16),
            (HBM, PACKED, BF16),
            (VMEM, PACKED_LAST, BF16),
            (VMEM, PACKED_LAST, BF16),
            (VMEM, (HQ, WIN), F32),
        ],
        [pltpu.VMEM((WIN, COLS), BF16)] * 2
        + [pltpu.VMEM(PACKED, BF16)] * 2
        + [pltpu.SMEM((HQ,), F32), DMA((2 * HK,)), DMA((2,)), DMA((2 * HK,)), DMA],
        cost(4, 2_500_000),
        length, sinks, k, v, q_first, d_first, q, d,
    )


def early_rows(parent, branch, level, sinks, q, d, k, v, lo, mid, hi, late_sink, copies):
    return call(
        early_kernel,
        "early_rows",
        [SMEM] * 3 + [HBM] + [VMEM] * 8,
        [
            (HBM, PACKED, BF16),
            (HBM, PACKED, BF16),
            (VMEM, PACKED_LAST, BF16),
            (VMEM, PACKED_LAST, BF16),
            (VMEM, (2 * WIN, KV), BF16),
            (RESULT, (copies, WIN), F32),
        ],
        [
            pltpu.VMEM((WIN, WIN), F32),
            pltpu.VMEM(PACKED, BF16),
            pltpu.VMEM(PACKED, BF16),
            pltpu.SMEM((HQ,), F32),
            DMA((2 * HK,)),
            DMA,
        ],
        cost(4, 5_000_000),
        parent, branch, level, sinks, q, d, k, v, lo, mid, hi, late_sink,
    )


def early_grads(parent, branch, q, d, keys, low_last, ds_last, low, ds):
    return call(
        early_grads_kernel,
        "early_grads",
        [SMEM] * 2 + [VMEM] * 5 + [HBM] * 2,
        [(HBM, (2 * WIN, COLS), BF16), (VMEM, (2, WIN, KV), F32), (VMEM, (2, WIN, KV), BF16)],
        [pltpu.VMEM((WIN, COLS), BF16), pltpu.VMEM(PACKED, BF16), pltpu.VMEM(PACKED, BF16), DMA((HK,)), DMA((2 * HK,))],
        SMALL,
        parent, branch, q, d, keys, low_last, ds_last, low, ds,
    )


def late_grads(length, q_last, d_last, k, own, lo, mid, hi, low_last, ds_last, q, d, low, ds, dq):
    return call(
        late_grads_kernel,
        "late_grads",
        [SMEM] + [VMEM] * 9 + [HBM] * 5,
        [(HBM, (2 * WIN, COLS), BF16), (RESULT, (2 * WIN, KV), BF16), (RESULT, (2 * WIN, KV), BF16)],
        [pltpu.VMEM((WIN, COLS), BF16)] * 3
        + [pltpu.VMEM(PACKED, BF16)] * 2
        + [DMA((HK,)), DMA((2 * HK,)), DMA((2 * HK,))],
        SMALL,
        length, q_last, d_last, k, own, lo, mid, hi, low_last, ds_last, q, d, low, ds, dq,
        aliases={14: 0},
    )


def add_up(rows, copies):
    return call(add_up_kernel, "add_up", [VMEM], [(VMEM, (copies, WIN), F32)], [], cost(100, 100), rows)[0]


def sent(rows, levels_on, by):
    levels, branches = lax.axis_size("ctx"), lax.axis_size("expert")
    pairs = [
        (level * branches + b, (level + levels_on) * branches + b + by)
        for level in range(levels)
        for b in range(branches)
        if 0 <= level + levels_on < levels and 0 <= b + by < branches
    ]
    return lax.ppermute(rows, ("ctx", "expert"), pairs)


def shards(query_rows, key_rows, value_rows, output_grad, sink_logits, parent_branch, segment_length):
    q = query_rows[0, 0, 0]
    k = key_rows[0, 0, 0]
    v = value_rows[0, 0, 0]
    d = output_grad[0, 0, 0]
    branch = lax.axis_index("expert").astype(jnp.int32).reshape(1)
    level = lax.axis_index("ctx").astype(jnp.int32).reshape(1)
    plane = lax.axis_size("dp") * lax.axis_size("ctx")
    experts = lax.axis_size("expert")

    k, v, tail, q_first, d_first = load(segment_length, k, v, q, d)
    tail, parent = lax.optimization_barrier((tail, parent_branch))
    length = segment_length
    mid, lo, hi = (sent(tail, 1, by) for by in (0, 1, -1))
    q_e, d_e, q_l3, d_l3, low_l, ds_l, low_l3, ds_l3, late_sink = late_rows(length, sink_logits, k, v, q_first, d_first, q, d)
    low_e, ds_e, low_e3, ds_e3, keys, sinks = early_rows(parent, branch, level, sink_logits, q_e, d_e, k, v, lo, mid, hi, late_sink, experts)

    column = lax.all_to_all(sinks, "expert", 0, 0, tiled=True)
    dq, early_own, tail = early_grads(parent, branch, q_e, d_e, keys, low_e3, ds_e3, low_e, ds_e)
    mid, lo, hi = (sent(tail, -1, by) for by in (0, 1, -1))
    everywhere = lax.all_to_all(add_up(column, plane), ("dp", "ctx"), 0, 0, tiled=True)
    dq, dk, dv = late_grads(length, q_l3, d_l3, k, early_own, lo, mid, hi, low_l3, ds_l3, q, d, low_l, ds_l, dq)
    everywhere, dk = lax.optimization_barrier((everywhere, dk))
    sink_grad = jnp.sum(everywhere, axis=0)[:HQ]
    return dq[None, None, None], dk[None, None, None], dv[None, None, None], sink_grad


def solution(mesh):
    part = P("dp", "ctx", "expert", None, None)
    scalar = P("dp", "ctx", "expert")
    return jax.shard_map(
        shards,
        mesh=mesh,
        in_specs=(part, part, part, part, P(), scalar, scalar),
        out_specs=(part, part, part, P()),
        check_vma=False,
    )
```

```python
import functools

import jax
import jax.numpy as jnp
from jax import lax
from jax.experimental import pallas as pl
from jax.experimental.pallas import tpu as pltpu
from jax.sharding import PartitionSpec as P

HQ = 32
HK = 4
HD = 64
WIN = 128
GROUP = HQ // HK
GCOLS = GROUP * HD
LOW = -1e30
F32 = jnp.float32
BF16 = jnp.bfloat16

NT = (((1,), (1,)), ((), ()))
TN = (((0,), (0,)), ((), ()))
NN = (((1,), (0,)), ((), ()))


def mm(a, b, dims):
    return lax.dot_general(a, b, dims, preferred_element_type=F32)


def upper():
    c = lax.broadcasted_iota(jnp.int32, (WIN, WIN), 0)
    r = lax.broadcasted_iota(jnp.int32, (WIN, WIN), 1)
    return c > r


def one_head(s, dp, sink, alive):
    top = jnp.maximum(jnp.max(s, axis=0, keepdims=True), sink)
    e = jnp.exp(s - top)
    sink_e = jnp.exp(sink - top)
    inv = 1.0 / (jnp.sum(e, axis=0, keepdims=True) + sink_e)
    if alive is not None:
        inv = jnp.where(alive, inv, 0.0)
    p = e * inv
    low = p.astype(BF16)
    delta = jnp.sum(low.astype(F32) * dp, axis=0, keepdims=True)
    ds = (p * (dp - delta)).astype(BF16)
    return low, ds, sink_e * inv * delta


def forward_group(sub, keys, values, q, d, seen_upper, sinks, first, bias, alive, low, ds, sink_out, sink_base):
    for pair in range(GROUP // 2):
        at = pair * 2 * HD
        q2 = jnp.concatenate([q[:, at : at + HD], q[:, at + HD : at + 2 * HD]], axis=0)
        d2 = jnp.concatenate([d[:, at : at + HD], d[:, at + HD : at + 2 * HD]], axis=0)
        s2 = mm(keys, q2, NT)
        dp2 = mm(values, d2, NT)
        for one in range(2):
            h = pair * 2 + one
            lanes = slice(one * WIN, (one + 1) * WIN)
            s_up = s2[:WIN, lanes]
            if bias is not None:
                s_up = s_up + bias
            s = jnp.where(seen_upper, s_up, s2[WIN:, lanes])
            dp = jnp.where(seen_upper, dp2[:WIN, lanes], dp2[WIN:, lanes])
            l_h, ds_h, sink_h = one_head(s, dp, sinks[pl.ds(first + h, 1), :], alive)
            cols = slice(h * WIN, (h + 1) * WIN)
            low[sub, :, cols] = l_h
            ds[sub, :, cols] = ds_h
            sink_out[pl.ds(sink_base + h, 1), :] = sink_h


def stacked(rows):
    return jnp.concatenate([rows[:, h * HD : (h + 1) * HD] for h in range(GROUP)], axis=0)


def upper_mask():
    mask = jnp.where(upper(), 1.0, 0.0).astype(BF16)
    return jnp.concatenate([mask] * GROUP, axis=1)


def query_side(keys, ds_all):
    dqt = mm(keys, ds_all, TN).astype(BF16)
    parts = []
    for pair in range(GROUP // 2):
        at = pair * 2 * WIN
        two = jnp.concatenate([dqt[:, at : at + WIN], dqt[:, at + WIN : at + 2 * WIN]], axis=0)
        parts.append(two.T)
    return jnp.concatenate(parts, axis=1)


def one_hot(hit):
    return jnp.where(hit, 1.0, 0.0).astype(BF16)


def start_all(copies):
    for copy in copies:
        copy.start()


def carried(g, sources, targets, sems):
    copies = [pltpu.make_async_copy(src.at[g], dst.at[g], sems.at[2 * g + n]) for n, (src, dst) in enumerate(zip(sources, targets))]
    start_all(copies)
    return copies


def columns_of(g, first, sources, targets, sems):
    cols = slice(g * GCOLS, (g + 1) * GCOLS)
    copies = [
        pltpu.make_async_copy(src.at[pl.ds(first, WIN), cols], dst.at[:, cols], sems.at[2 * g + n])
        for n, (src, dst) in enumerate(zip(sources, targets))
    ]
    start_all(copies)
    return copies


def load_kernel(length, sinks_in, k_in, v_in, q_in, d_in, k_ref, v_ref, tail_ref, q_first, d_first, sinks_ref, sinks, sems, first_sems, sink_sem):
    copies = [pltpu.make_async_copy(src, dst, sems.at[n]) for n, (src, dst) in enumerate(((k_in, k_ref), (v_in, v_ref)))]
    start_all(copies)
    sinks_copy = pltpu.make_async_copy(sinks_in, sinks, sink_sem)
    sinks_copy.start()
    firsts = columns_of(0, WIN, (q_in, d_in), (q_first, d_first), first_sems)
    c = lax.broadcasted_iota(jnp.int32, (WIN, 2 * WIN), 0)
    j = lax.broadcasted_iota(jnp.int32, (WIN, 2 * WIN), 1)
    pick = one_hot(j == c + (length[0, 0, 0] - WIN))
    for copy, ref, part in zip(copies, (k_ref, v_ref), range(2)):
        copy.wait()
        tail_ref[part] = mm(pick, ref[...], NN).astype(BF16)
    sinks_copy.wait()
    for h in range(HQ):
        sinks_ref[pl.ds(h, 1), :] = jnp.full((1, WIN), sinks[h], F32)
    for copy in firsts:
        copy.wait()


def late_kernel(length, sinks, k_ref, v_ref, q_first, d_first, q_in, d_in, q_early, d_early, q_last, d_last, low_out, ds_out, low_last, ds_last, sink_ref, q_ref, d_ref, low, ds, sems, early_sems, out_sems):
    came = {g: columns_of(g, WIN, (q_in, d_in), (q_ref, d_ref), sems) for g in range(1, LAST)}
    cols = slice(LAST * GCOLS, HK * GCOLS)
    came[LAST] = [
        pltpu.make_async_copy(src.at[pl.ds(WIN, WIN), cols], dst, sems.at[2 * LAST + n])
        for n, (src, dst) in enumerate(((q_in, q_last), (d_in, d_last)))
    ]
    brought = [
        pltpu.make_async_copy(src.at[pl.ds(0, WIN), :], dst, early_sems.at[n])
        for n, (src, dst) in enumerate(((q_in, q_early), (d_in, d_early)))
    ]
    start_all(came[LAST] + brought)
    seen_upper = upper()
    alive = lax.broadcasted_iota(jnp.int32, (1, WIN), 1) < length[0, 0, 0] - WIN
    written = []
    for g in range(HK):
        cols = slice(g * GCOLS, (g + 1) * GCOLS)
        kv = slice(g * HD, (g + 1) * HD)
        for copy in came.get(g, ()):
            copy.wait()
        if g == 0:
            q, d = q_first[...], d_first[...]
        elif g < LAST:
            q, d = q_ref[:, cols], d_ref[:, cols]
        else:
            q, d = q_last[...], d_last[...]
        to = (g, low, ds) if g < LAST else (0, low_last, ds_last)
        keys = k_ref[:, kv] * (HD**-0.5)
        forward_group(to[0], keys, v_ref[:, kv], q, d, seen_upper, sinks, g * GROUP, None, alive, to[1], to[2], sink_ref, g * GROUP)
        if g < LAST:
            written += carried(g, (low, ds), (low_out, ds_out), out_sems)
    for copy in brought + written:
        copy.wait()


def early_kernel(parent, branch, level, sinks, q_ref, d_ref, k_ref, v_ref, lo, mid, hi, late_sink, low_out, ds_out, low_last, ds_last, keys_ref, sink_ref, sink_rows, low, ds, out_sems):
    slot = parent[0, 0, 0] - branch[0] + 1
    bias = jnp.where(level[0] > 0, 0.0, LOW)
    seen_upper = upper()
    sink_rows[HQ:, :] = jnp.zeros((WIN - HQ, WIN), F32)
    written = []
    tail = jnp.where(slot == 0, lo[...], jnp.where(slot == 1, mid[...], hi[...]))
    for g in range(HK):
        cols = slice(g * GCOLS, (g + 1) * GCOLS)
        kv = slice(g * HD, (g + 1) * HD)
        keys = jnp.concatenate([tail[0, :, kv], k_ref[:WIN, kv]], axis=0) * (HD**-0.5)
        values = jnp.concatenate([tail[1, :, kv], v_ref[:WIN, kv]], axis=0)
        keys_ref[:, kv] = keys
        to = (g, low, ds) if g < FAR else (g - FAR, low_last, ds_last)
        forward_group(to[0], keys, values, q_ref[:, cols], d_ref[:, cols], seen_upper, sinks, g * GROUP, bias, None, to[1], to[2], sink_rows, g * GROUP)
        if g < FAR:
            written += carried(g, (low, ds), (low_out, ds_out), out_sems)
    sink_rows[:HQ, :] = sink_rows[:HQ, :] + late_sink[...]
    total = -jnp.sum(sink_rows[...].T, axis=0, keepdims=True)
    sink_ref[...] = jnp.broadcast_to(total, sink_ref.shape)
    for copy in written:
        copy.wait()


def one_side(keys, q, d, low, ds, mask):
    ds_up = ds * mask
    low_up = low * mask
    ds_all = jnp.concatenate([ds_up, ds - ds_up], axis=0)
    low_all = jnp.concatenate([low_up, low - low_up], axis=0)
    dk = mm(ds_all, stacked(q), NN) * (HD**-0.5)
    dv = mm(low_all, stacked(d), NN)
    return query_side(keys, ds_all), dk, dv


def early_grads_kernel(parent, branch, q_ref, d_ref, keys_ref, low_last, ds_last, low_in, ds_in, dq_out, own_ref, tail_ref, dq_ref, low, ds, sems, in_sems):
    came = [carried(g, (low_in, ds_in), (low, ds), in_sems) for g in range(FAR)]
    mask = upper_mask()
    flag = (parent[0, 0, 0] - branch[0] + 2).astype(F32)
    row = lax.broadcasted_iota(jnp.int32, (WIN, HD), 0)
    rows = slice(0, WIN)
    copies = []
    for g in tuple(range(FAR, HK)) + tuple(range(FAR)):
        cols = slice(g * GCOLS, (g + 1) * GCOLS)
        kv = slice(g * HD, (g + 1) * HD)
        if g < FAR:
            for copy in came[g]:
                copy.wait()
        low_g, ds_g = (low[g], ds[g]) if g < FAR else (low_last[g - FAR], ds_last[g - FAR])
        dq_ref[:, cols], dk, dv = one_side(keys_ref[:, kv], q_ref[:, cols], d_ref[:, cols], low_g, ds_g, mask)
        copies.append(pltpu.make_async_copy(dq_ref.at[:, cols], dq_out.at[rows, cols], sems.at[g]))
        copies[-1].start()
        tail_ref[0, :, kv] = jnp.where(row == 0, flag, dk[:WIN]).astype(BF16)
        tail_ref[1, :, kv] = dv[:WIN].astype(BF16)
        own_ref[0, :, kv] = dk[WIN:]
        own_ref[1, :, kv] = dv[WIN:]
    for copy in copies:
        copy.wait()


def late_grads_kernel(length, q_last, d_last, k_ref, own, lo, mid, hi, low_last, ds_last, q_in, d_in, low_in, ds_in, dq_in, dq_out, dk_ref, dv_ref, dq_ref, q_ref, d_ref, low, ds, sems, in_sems, q_sems):
    del dq_in
    came = []
    for g in range(LAST):
        came.append(carried(g, (low_in, ds_in), (low, ds), in_sems) + columns_of(g, WIN, (q_in, d_in), (q_ref, d_ref), q_sems))
    mask = upper_mask()
    j = lax.broadcasted_iota(jnp.int32, (2 * WIN, WIN), 0)
    c = lax.broadcasted_iota(jnp.int32, (2 * WIN, WIN), 1)
    put = (j == c + (length[0, 0, 0] - WIN)) & (c > 0)
    picked = []
    for child, mark in ((lo, 3.0), (mid, 2.0), (hi, 1.0)):
        mine = jnp.max(child[0, :16, :WIN].astype(F32)[0:1, 0:1]) == mark
        picked.append(one_hot(put & mine))
    pick = jnp.concatenate(picked, axis=1)
    sums = []
    for part in range(2):
        children = jnp.concatenate([lo[part], mid[part], hi[part]], axis=0)
        sums.append(mm(pick, children, NN))
    rows = slice(WIN, 2 * WIN)
    copies = []
    for g in (LAST,) + tuple(range(LAST)):
        cols = slice(g * GCOLS, (g + 1) * GCOLS)
        kv = slice(g * HD, (g + 1) * HD)
        if g < LAST:
            for copy in came[g]:
                copy.wait()
        if g < LAST:
            q_g, d_g, low_g, ds_g = q_ref[:, cols], d_ref[:, cols], low[g], ds[g]
        else:
            q_g, d_g, low_g, ds_g = q_last[...], d_last[...], low_last[0], ds_last[0]
        dq_ref[:, cols], dk, dv = one_side(k_ref[:, kv] * (HD**-0.5), q_g, d_g, low_g, ds_g, mask)
        copies.append(pltpu.make_async_copy(dq_ref.at[:, cols], dq_out.at[rows, cols], sems.at[g]))
        copies[-1].start()
        for part, (late, out) in enumerate(((dk, dk_ref), (dv, dv_ref))):
            total = late + sums[part][:, kv]
            out[:WIN, kv] = (total[:WIN] + own[part, :, kv]).astype(BF16)
            out[WIN:, kv] = total[WIN:].astype(BF16)
    for copy in copies:
        copy.wait()


def add_up_kernel(rows, out):
    out[...] = jnp.broadcast_to(jnp.sum(rows[...], axis=0, keepdims=True), out.shape)


SMEM = pl.BlockSpec(memory_space=pltpu.SMEM)
VMEM = pl.BlockSpec(memory_space=pltpu.VMEM)
RESULT = pl.BlockSpec(memory_space=pltpu.VMEM)
HBM = pl.BlockSpec(memory_space=pltpu.HBM)
PARAMS = pltpu.CompilerParams(vmem_limit_bytes=40 * 1024 * 1024)
KV = HK * HD
COLS = HQ * HD
DMA = pltpu.SemaphoreType.DMA
LAST = HK - 1
PACKED = (LAST, WIN, GROUP * WIN)
PACKED_LAST = (1, WIN, GROUP * WIN)
FAR = 3
PACKED_FAR = (FAR, WIN, GROUP * WIN)
PACKED_NEAR = (HK - FAR, WIN, GROUP * WIN)


def shaped(shape, dtype):
    return jax.ShapeDtypeStruct(shape, dtype)


def cost(products, size):
    return pl.CostEstimate(flops=products * 2 * 32 * 128 * 256 * 64, bytes_accessed=size, transcendentals=0)


SMALL = pl.CostEstimate(flops=1000, bytes_accessed=1000, transcendentals=0)


def held(operand, spec):
    space = {id(VMEM): pltpu.VMEM, id(HBM): pltpu.HBM}.get(id(spec), pl.ANY)
    return pltpu.with_memory_space_constraint(operand, space)


def made(spec, shape, dtype):
    space = {id(VMEM): pltpu.VMEM, id(HBM): pltpu.HBM}.get(id(spec), shaped)
    return space(shape, dtype)


def call(kernel, name, ins, outs, scratch, estimate, *operands, aliases=None):
    operands = [held(operand, spec) for operand, spec in zip(operands, ins)]
    return pl.pallas_call(
        kernel,
        in_specs=ins,
        out_specs=tuple(spec for spec, _, _ in outs),
        out_shape=tuple(made(*out) for out in outs),
        scratch_shapes=scratch,
        compiler_params=PARAMS,
        input_output_aliases=aliases or {},
        cost_estimate=estimate,
        name=name,
    )(*operands)


def load(length, sinks, k, v, q, d):
    return call(
        load_kernel,
        "load",
        [SMEM] + [HBM] * 5,
        [
            (VMEM, (2 * WIN, KV), BF16),
            (VMEM, (2 * WIN, KV), BF16),
            (VMEM, (2, WIN, KV), BF16),
            (VMEM, (WIN, GCOLS), BF16),
            (VMEM, (WIN, GCOLS), BF16),
            (VMEM, (HQ, WIN), F32),
        ],
        [pltpu.SMEM((HQ,), F32), DMA((2,)), DMA((2,)), DMA],
        cost(1, 400_000),
        length, sinks, k, v, q, d,
    )


def late_rows(length, sinks, k, v, q_first, d_first, q, d):
    return call(
        late_kernel,
        "late_rows",
        [SMEM] + [VMEM] * 5 + [HBM] * 2,
        [
            (VMEM, (WIN, COLS), BF16),
            (VMEM, (WIN, COLS), BF16),
            (VMEM, (WIN, GCOLS), BF16),
            (VMEM, (WIN, GCOLS), BF16),
            (HBM, PACKED, BF16),
            (HBM, PACKED, BF16),
            (VMEM, PACKED_LAST, BF16),
            (VMEM, PACKED_LAST, BF16),
            (VMEM, (HQ, WIN), F32),
        ],
        [pltpu.VMEM((WIN, COLS), BF16)] * 2
        + [pltpu.VMEM(PACKED, BF16)] * 2
        + [DMA((2 * HK,)), DMA((2,)), DMA((2 * HK,))],
        cost(4, 2_500_000),
        length, sinks, k, v, q_first, d_first, q, d,
    )


def early_rows(parent, branch, level, sinks, q, d, k, v, lo, mid, hi, late_sink, copies):
    return call(
        early_kernel,
        "early_rows",
        [SMEM] * 3 + [VMEM] * 9,
        [
            (HBM, PACKED_FAR, BF16),
            (HBM, PACKED_FAR, BF16),
            (VMEM, PACKED_NEAR, BF16),
            (VMEM, PACKED_NEAR, BF16),
            (VMEM, (2 * WIN, KV), BF16),
            (RESULT, (copies, WIN), F32),
        ],
        [
            pltpu.VMEM((WIN, WIN), F32),
            pltpu.VMEM(PACKED_FAR, BF16),
            pltpu.VMEM(PACKED_FAR, BF16),
            DMA((2 * FAR,)),
        ],
        cost(4, 5_000_000),
        parent, branch, level, sinks, q, d, k, v, lo, mid, hi, late_sink,
    )


def early_grads(parent, branch, q, d, keys, low_last, ds_last, low, ds):
    return call(
        early_grads_kernel,
        "early_grads",
        [SMEM] * 2 + [VMEM] * 5 + [HBM] * 2,
        [(HBM, (2 * WIN, COLS), BF16), (VMEM, (2, WIN, KV), F32), (VMEM, (2, WIN, KV), BF16)],
        [pltpu.VMEM((WIN, COLS), BF16), pltpu.VMEM(PACKED_FAR, BF16), pltpu.VMEM(PACKED_FAR, BF16), DMA((HK,)), DMA((2 * FAR,))],
        SMALL,
        parent, branch, q, d, keys, low_last, ds_last, low, ds,
    )


def late_grads(length, q_last, d_last, k, own, lo, mid, hi, low_last, ds_last, q, d, low, ds, dq):
    return call(
        late_grads_kernel,
        "late_grads",
        [SMEM] + [VMEM] * 9 + [HBM] * 5,
        [(HBM, (2 * WIN, COLS), BF16), (RESULT, (2 * WIN, KV), BF16), (RESULT, (2 * WIN, KV), BF16)],
        [pltpu.VMEM((WIN, COLS), BF16)] * 3
        + [pltpu.VMEM(PACKED, BF16)] * 2
        + [DMA((HK,)), DMA((2 * HK,)), DMA((2 * HK,))],
        SMALL,
        length, q_last, d_last, k, own, lo, mid, hi, low_last, ds_last, q, d, low, ds, dq,
        aliases={14: 0},
    )


def add_up(rows, copies):
    return call(add_up_kernel, "add_up", [VMEM], [(VMEM, (copies, WIN), F32)], [], cost(100, 100), rows)[0]


def sent(rows, levels_on, by):
    levels, branches = lax.axis_size("ctx"), lax.axis_size("expert")
    pairs = [
        (level * branches + b, (level + levels_on) * branches + b + by)
        for level in range(levels)
        for b in range(branches)
        if 0 <= level + levels_on < levels and 0 <= b + by < branches
    ]
    return lax.ppermute(rows, ("ctx", "expert"), pairs)


def shards(query_rows, key_rows, value_rows, output_grad, sink_logits, parent_branch, segment_length):
    q = query_rows[0, 0, 0]
    k = key_rows[0, 0, 0]
    v = value_rows[0, 0, 0]
    d = output_grad[0, 0, 0]
    branch = lax.axis_index("expert").astype(jnp.int32).reshape(1)
    level = lax.axis_index("ctx").astype(jnp.int32).reshape(1)
    plane = lax.axis_size("dp") * lax.axis_size("ctx")
    experts = lax.axis_size("expert")

    k, v, tail, q_first, d_first, sink_rows = load(segment_length, sink_logits, k, v, q, d)
    length = segment_length
    mid, lo, hi = (sent(tail, 1, by) for by in (0, 1, -1))
    q_e, d_e, q_l3, d_l3, low_l, ds_l, low_l3, ds_l3, late_sink = late_rows(length, sink_rows, k, v, q_first, d_first, q, d)
    late_sink, parent = lax.optimization_barrier((late_sink, parent_branch))
    low_e, ds_e, low_e3, ds_e3, keys, sinks = early_rows(parent, branch, level, sink_rows, q_e, d_e, k, v, lo, mid, hi, late_sink, experts)

    column = lax.all_to_all(sinks, "expert", 0, 0, tiled=True)
    dq, early_own, tail = early_grads(parent, branch, q_e, d_e, keys, low_e3, ds_e3, low_e, ds_e)
    mid, lo, hi = (sent(tail, -1, by) for by in (0, 1, -1))
    everywhere = lax.all_to_all(add_up(column, plane), ("dp", "ctx"), 0, 0, tiled=True)
    dq, dk, dv = late_grads(length, q_l3, d_l3, k, early_own, lo, mid, hi, low_l3, ds_l3, q, d, low_l, ds_l, dq)
    everywhere, dk = lax.optimization_barrier((everywhere, dk))
    sink_grad = jnp.sum(everywhere, axis=0)[:HQ]
    return dq[None, None, None], dk[None, None, None], dv[None, None, None], sink_grad


def solution(mesh):
    part = P("dp", "ctx", "expert", None, None)
    scalar = P("dp", "ctx", "expert")
    return jax.shard_map(
        shards,
        mesh=mesh,
        in_specs=(part, part, part, part, P(), scalar, scalar),
        out_specs=(part, part, part, P()),
        check_vma=False,
    )
```

```python
import functools

import jax
import jax.numpy as jnp
from jax import lax
from jax.experimental import pallas as pl
from jax.experimental.pallas import tpu as pltpu
from jax.sharding import PartitionSpec as P

HQ = 32
HK = 4
HD = 64
WIN = 128
GROUP = HQ // HK
GCOLS = GROUP * HD
LOW = -1e30
F32 = jnp.float32
BF16 = jnp.bfloat16

NT = (((1,), (1,)), ((), ()))
TN = (((0,), (0,)), ((), ()))
NN = (((1,), (0,)), ((), ()))


def mm(a, b, dims):
    return lax.dot_general(a, b, dims, preferred_element_type=F32)


def upper():
    c = lax.broadcasted_iota(jnp.int32, (WIN, WIN), 0)
    r = lax.broadcasted_iota(jnp.int32, (WIN, WIN), 1)
    return c > r


def one_head(s, dp, sink, alive):
    top = jnp.maximum(jnp.max(s, axis=0, keepdims=True), sink)
    e = jnp.exp(s - top)
    sink_e = jnp.exp(sink - top)
    inv = 1.0 / (jnp.sum(e, axis=0, keepdims=True) + sink_e)
    if alive is not None:
        inv = jnp.where(alive, inv, 0.0)
    p = e * inv
    low = p.astype(BF16)
    delta = jnp.sum(low.astype(F32) * dp, axis=0, keepdims=True)
    ds = (p * (dp - delta)).astype(BF16)
    return low, ds, sink_e * inv * delta


def forward_group(sub, keys, values, q, d, seen_upper, sinks, first, bias, alive, low, ds, sink_out, sink_base):
    for pair in range(GROUP // 2):
        at = pair * 2 * HD
        q2 = jnp.concatenate([q[:, at : at + HD], q[:, at + HD : at + 2 * HD]], axis=0)
        d2 = jnp.concatenate([d[:, at : at + HD], d[:, at + HD : at + 2 * HD]], axis=0)
        s2 = mm(keys, q2, NT)
        dp2 = mm(values, d2, NT)
        for one in range(2):
            h = pair * 2 + one
            lanes = slice(one * WIN, (one + 1) * WIN)
            s_up = s2[:WIN, lanes]
            if bias is not None:
                s_up = s_up + bias
            s = jnp.where(seen_upper, s_up, s2[WIN:, lanes])
            dp = jnp.where(seen_upper, dp2[:WIN, lanes], dp2[WIN:, lanes])
            l_h, ds_h, sink_h = one_head(s, dp, sinks[pl.ds(first + h, 1), :], alive)
            cols = slice(h * WIN, (h + 1) * WIN)
            low[sub, :, cols] = l_h
            ds[sub, :, cols] = ds_h
            sink_out[pl.ds(sink_base + h, 1), :] = sink_h


def stacked(rows):
    return jnp.concatenate([rows[:, h * HD : (h + 1) * HD] for h in range(GROUP)], axis=0)


def upper_mask():
    mask = jnp.where(upper(), 1.0, 0.0).astype(BF16)
    return jnp.concatenate([mask] * GROUP, axis=1)


def query_side(keys, ds_all):
    dqt = mm(keys, ds_all, TN).astype(BF16)
    parts = []
    for pair in range(GROUP // 2):
        at = pair * 2 * WIN
        two = jnp.concatenate([dqt[:, at : at + WIN], dqt[:, at + WIN : at + 2 * WIN]], axis=0)
        parts.append(two.T)
    return jnp.concatenate(parts, axis=1)


def one_hot(hit):
    return jnp.where(hit, 1.0, 0.0).astype(BF16)


def start_all(copies):
    for copy in copies:
        copy.start()


def carried(g, sources, targets, sems):
    copies = [pltpu.make_async_copy(src.at[g], dst.at[g], sems.at[2 * g + n]) for n, (src, dst) in enumerate(zip(sources, targets))]
    start_all(copies)
    return copies


def columns_of(g, first, sources, targets, sems):
    cols = slice(g * GCOLS, (g + 1) * GCOLS)
    copies = [
        pltpu.make_async_copy(src.at[pl.ds(first, WIN), cols], dst.at[:, cols], sems.at[2 * g + n])
        for n, (src, dst) in enumerate(zip(sources, targets))
    ]
    start_all(copies)
    return copies


def load_kernel(length, sinks_in, k_in, v_in, q_in, d_in, k_ref, v_ref, tail_ref, q_first, d_first, sinks_ref, sinks, sems, first_sems, sink_sem):
    copies = [pltpu.make_async_copy(src, dst, sems.at[n]) for n, (src, dst) in enumerate(((k_in, k_ref), (v_in, v_ref)))]
    start_all(copies)
    sinks_copy = pltpu.make_async_copy(sinks_in, sinks, sink_sem)
    sinks_copy.start()
    firsts = columns_of(0, WIN, (q_in, d_in), (q_first, d_first), first_sems)
    c = lax.broadcasted_iota(jnp.int32, (WIN, 2 * WIN), 0)
    j = lax.broadcasted_iota(jnp.int32, (WIN, 2 * WIN), 1)
    pick = one_hot(j == c + (length[0, 0, 0] - WIN))
    for copy, ref, part in zip(copies, (k_ref, v_ref), range(2)):
        copy.wait()
        tail_ref[part] = mm(pick, ref[...], NN).astype(BF16)
    sinks_copy.wait()
    for h in range(HQ):
        sinks_ref[pl.ds(h, 1), :] = jnp.full((1, WIN), sinks[h], F32)
    for copy in firsts:
        copy.wait()


def late_kernel(length, sinks, k_ref, v_ref, q_first, d_first, q_in, d_in, q_early, d_early, q_last, d_last, low_out, ds_out, low_last, ds_last, sink_ref, q_ref, d_ref, low, ds, sems, early_sems, out_sems):
    came = {g: columns_of(g, WIN, (q_in, d_in), (q_ref, d_ref), sems) for g in range(1, LAST)}
    cols = slice(LAST * GCOLS, HK * GCOLS)
    came[LAST] = [
        pltpu.make_async_copy(src.at[pl.ds(WIN, WIN), cols], dst, sems.at[2 * LAST + n])
        for n, (src, dst) in enumerate(((q_in, q_last), (d_in, d_last)))
    ]
    brought = [
        pltpu.make_async_copy(src.at[pl.ds(0, WIN), :], dst, early_sems.at[n])
        for n, (src, dst) in enumerate(((q_in, q_early), (d_in, d_early)))
    ]
    start_all(came[LAST] + brought)
    seen_upper = upper()
    alive = lax.broadcasted_iota(jnp.int32, (1, WIN), 1) < length[0, 0, 0] - WIN
    written = []
    for g in range(HK):
        cols = slice(g * GCOLS, (g + 1) * GCOLS)
        kv = slice(g * HD, (g + 1) * HD)
        for copy in came.get(g, ()):
            copy.wait()
        if g == 0:
            q, d = q_first[...], d_first[...]
        elif g < LAST:
            q, d = q_ref[:, cols], d_ref[:, cols]
        else:
            q, d = q_last[...], d_last[...]
        to = (g, low, ds) if g < LAST else (0, low_last, ds_last)
        keys = k_ref[:, kv] * (HD**-0.5)
        forward_group(to[0], keys, v_ref[:, kv], q, d, seen_upper, sinks, g * GROUP, None, alive, to[1], to[2], sink_ref, g * GROUP)
        if g < LAST:
            written += carried(g, (low, ds), (low_out, ds_out), out_sems)
    for copy in brought + written:
        copy.wait()


def early_kernel(parent, branch, level, sinks, q_ref, d_ref, k_ref, v_ref, lo, mid, hi, late_sink, low_out, ds_out, low_last, ds_last, keys_ref, sink_ref, sink_rows, low, ds, out_sems):
    slot = parent[0, 0, 0] - branch[0] + 1
    bias = jnp.where(level[0] > 0, 0.0, LOW)
    seen_upper = upper()
    sink_rows[HQ:, :] = jnp.zeros((WIN - HQ, WIN), F32)
    written = []
    tail = jnp.where(slot == 0, lo[...], jnp.where(slot == 1, mid[...], hi[...]))
    for g in range(HK):
        cols = slice(g * GCOLS, (g + 1) * GCOLS)
        kv = slice(g * HD, (g + 1) * HD)
        keys = jnp.concatenate([tail[0, :, kv], k_ref[:WIN, kv]], axis=0) * (HD**-0.5)
        values = jnp.concatenate([tail[1, :, kv], v_ref[:WIN, kv]], axis=0)
        keys_ref[:, kv] = keys
        to = (g, low, ds) if g < FAR else (g - FAR, low_last, ds_last)
        forward_group(to[0], keys, values, q_ref[:, cols], d_ref[:, cols], seen_upper, sinks, g * GROUP, bias, None, to[1], to[2], sink_rows, g * GROUP)
        if g < FAR:
            written += carried(g, (low, ds), (low_out, ds_out), out_sems)
    sink_rows[:HQ, :] = sink_rows[:HQ, :] + late_sink[...]
    total = -jnp.sum(sink_rows[...].T, axis=0, keepdims=True)
    sink_ref[...] = jnp.broadcast_to(total, sink_ref.shape)
    for copy in written:
        copy.wait()


def one_side(keys, q, d, low, ds, mask, send):
    ds_up = ds * mask
    low_up = low * mask
    ds_all = jnp.concatenate([ds_up, ds - ds_up], axis=0)
    low_all = jnp.concatenate([low_up, low - low_up], axis=0)
    send(query_side(keys, ds_all))
    dk = mm(ds_all, stacked(q), NN) * (HD**-0.5)
    dv = mm(low_all, stacked(d), NN)
    return dk, dv


def early_grads_kernel(parent, branch, q_ref, d_ref, keys_ref, low_last, ds_last, low_in, ds_in, dq_out, own_ref, tail_ref, dq_ref, low, ds, sems, in_sems):
    came = [carried(g, (low_in, ds_in), (low, ds), in_sems) for g in range(FAR)]
    mask = upper_mask()
    flag = (parent[0, 0, 0] - branch[0] + 2).astype(F32)
    row = lax.broadcasted_iota(jnp.int32, (WIN, HD), 0)
    rows = slice(0, WIN)
    copies = []
    for g in tuple(range(FAR, HK)) + tuple(range(FAR)):
        cols = slice(g * GCOLS, (g + 1) * GCOLS)
        kv = slice(g * HD, (g + 1) * HD)
        if g < FAR:
            for copy in came[g]:
                copy.wait()
        low_g, ds_g = (low[g], ds[g]) if g < FAR else (low_last[g - FAR], ds_last[g - FAR])

        def send(dq, g=g, cols=cols):
            dq_ref[:, cols] = dq
            copies.append(pltpu.make_async_copy(dq_ref.at[:, cols], dq_out.at[rows, cols], sems.at[g]))
            copies[-1].start()

        dk, dv = one_side(keys_ref[:, kv], q_ref[:, cols], d_ref[:, cols], low_g, ds_g, mask, send)
        tail_ref[0, :, kv] = jnp.where(row == 0, flag, dk[:WIN]).astype(BF16)
        tail_ref[1, :, kv] = dv[:WIN].astype(BF16)
        own_ref[0, :, kv] = dk[WIN:]
        own_ref[1, :, kv] = dv[WIN:]
    for copy in copies:
        copy.wait()


def late_grads_kernel(length, q_last, d_last, k_ref, own, lo, mid, hi, low_last, ds_last, q_in, d_in, low_in, ds_in, dq_in, dq_out, dk_ref, dv_ref, dq_ref, q_ref, d_ref, low, ds, sems, in_sems, q_sems):
    del dq_in
    came = []
    for g in range(LAST):
        came.append(carried(g, (low_in, ds_in), (low, ds), in_sems) + columns_of(g, WIN, (q_in, d_in), (q_ref, d_ref), q_sems))
    mask = upper_mask()
    j = lax.broadcasted_iota(jnp.int32, (2 * WIN, WIN), 0)
    c = lax.broadcasted_iota(jnp.int32, (2 * WIN, WIN), 1)
    put = (j == c + (length[0, 0, 0] - WIN)) & (c > 0)
    picked = []
    for child, mark in ((lo, 3.0), (mid, 2.0), (hi, 1.0)):
        mine = jnp.max(child[0, :16, :WIN].astype(F32)[0:1, 0:1]) == mark
        picked.append(one_hot(put & mine))
    pick = jnp.concatenate(picked, axis=1)
    sums = []
    for part in range(2):
        children = jnp.concatenate([lo[part], mid[part], hi[part]], axis=0)
        sums.append(mm(pick, children, NN))
    rows = slice(WIN, 2 * WIN)
    copies = []
    for g in (LAST,) + tuple(range(LAST)):
        cols = slice(g * GCOLS, (g + 1) * GCOLS)
        kv = slice(g * HD, (g + 1) * HD)
        if g < LAST:
            for copy in came[g]:
                copy.wait()
        if g < LAST:
            q_g, d_g, low_g, ds_g = q_ref[:, cols], d_ref[:, cols], low[g], ds[g]
        else:
            q_g, d_g, low_g, ds_g = q_last[...], d_last[...], low_last[0], ds_last[0]

        def send(dq, g=g, cols=cols):
            dq_ref[:, cols] = dq
            copies.append(pltpu.make_async_copy(dq_ref.at[:, cols], dq_out.at[rows, cols], sems.at[g]))
            copies[-1].start()

        dk, dv = one_side(k_ref[:, kv] * (HD**-0.5), q_g, d_g, low_g, ds_g, mask, send)
        for part, (late, out) in enumerate(((dk, dk_ref), (dv, dv_ref))):
            total = late + sums[part][:, kv]
            out[:WIN, kv] = (total[:WIN] + own[part, :, kv]).astype(BF16)
            out[WIN:, kv] = total[WIN:].astype(BF16)
    for copy in copies:
        copy.wait()


def add_up_kernel(rows, out):
    out[...] = jnp.broadcast_to(jnp.sum(rows[...], axis=0, keepdims=True), out.shape)


SMEM = pl.BlockSpec(memory_space=pltpu.SMEM)
VMEM = pl.BlockSpec(memory_space=pltpu.VMEM)
RESULT = pl.BlockSpec(memory_space=pltpu.VMEM)
HBM = pl.BlockSpec(memory_space=pltpu.HBM)
PARAMS = pltpu.CompilerParams(vmem_limit_bytes=40 * 1024 * 1024)
KV = HK * HD
COLS = HQ * HD
DMA = pltpu.SemaphoreType.DMA
LAST = HK - 1
PACKED = (LAST, WIN, GROUP * WIN)
PACKED_LAST = (1, WIN, GROUP * WIN)
FAR = 3
PACKED_FAR = (FAR, WIN, GROUP * WIN)
PACKED_NEAR = (HK - FAR, WIN, GROUP * WIN)


def shaped(shape, dtype):
    return jax.ShapeDtypeStruct(shape, dtype)


def cost(products, size):
    return pl.CostEstimate(flops=products * 2 * 32 * 128 * 256 * 64, bytes_accessed=size, transcendentals=0)


SMALL = pl.CostEstimate(flops=1000, bytes_accessed=1000, transcendentals=0)


def held(operand, spec):
    space = {id(VMEM): pltpu.VMEM, id(HBM): pltpu.HBM}.get(id(spec), pl.ANY)
    return pltpu.with_memory_space_constraint(operand, space)


def made(spec, shape, dtype):
    space = {id(VMEM): pltpu.VMEM, id(HBM): pltpu.HBM}.get(id(spec), shaped)
    return space(shape, dtype)


def call(kernel, name, ins, outs, scratch, estimate, *operands, aliases=None):
    operands = [held(operand, spec) for operand, spec in zip(operands, ins)]
    return pl.pallas_call(
        kernel,
        in_specs=ins,
        out_specs=tuple(spec for spec, _, _ in outs),
        out_shape=tuple(made(*out) for out in outs),
        scratch_shapes=scratch,
        compiler_params=PARAMS,
        input_output_aliases=aliases or {},
        cost_estimate=estimate,
        name=name,
    )(*operands)


def load(length, sinks, k, v, q, d):
    return call(
        load_kernel,
        "load",
        [SMEM] + [HBM] * 5,
        [
            (VMEM, (2 * WIN, KV), BF16),
            (VMEM, (2 * WIN, KV), BF16),
            (VMEM, (2, WIN, KV), BF16),
            (VMEM, (WIN, GCOLS), BF16),
            (VMEM, (WIN, GCOLS), BF16),
            (VMEM, (HQ, WIN), F32),
        ],
        [pltpu.SMEM((HQ,), F32), DMA((2,)), DMA((2,)), DMA],
        cost(1, 400_000),
        length, sinks, k, v, q, d,
    )


def late_rows(length, sinks, k, v, q_first, d_first, q, d):
    return call(
        late_kernel,
        "late_rows",
        [SMEM] + [VMEM] * 5 + [HBM] * 2,
        [
            (VMEM, (WIN, COLS), BF16),
            (VMEM, (WIN, COLS), BF16),
            (VMEM, (WIN, GCOLS), BF16),
            (VMEM, (WIN, GCOLS), BF16),
            (HBM, PACKED, BF16),
            (HBM, PACKED, BF16),
            (VMEM, PACKED_LAST, BF16),
            (VMEM, PACKED_LAST, BF16),
            (VMEM, (HQ, WIN), F32),
        ],
        [pltpu.VMEM((WIN, COLS), BF16)] * 2
        + [pltpu.VMEM(PACKED, BF16)] * 2
        + [DMA((2 * HK,)), DMA((2,)), DMA((2 * HK,))],
        cost(4, 2_500_000),
        length, sinks, k, v, q_first, d_first, q, d,
    )


def early_rows(parent, branch, level, sinks, q, d, k, v, lo, mid, hi, late_sink, copies):
    return call(
        early_kernel,
        "early_rows",
        [SMEM] * 3 + [VMEM] * 9,
        [
            (HBM, PACKED_FAR, BF16),
            (HBM, PACKED_FAR, BF16),
            (VMEM, PACKED_NEAR, BF16),
            (VMEM, PACKED_NEAR, BF16),
            (VMEM, (2 * WIN, KV), BF16),
            (RESULT, (copies, WIN), F32),
        ],
        [
            pltpu.VMEM((WIN, WIN), F32),
            pltpu.VMEM(PACKED_FAR, BF16),
            pltpu.VMEM(PACKED_FAR, BF16),
            DMA((2 * FAR,)),
        ],
        cost(4, 5_000_000),
        parent, branch, level, sinks, q, d, k, v, lo, mid, hi, late_sink,
    )


def early_grads(parent, branch, q, d, keys, low_last, ds_last, low, ds):
    return call(
        early_grads_kernel,
        "early_grads",
        [SMEM] * 2 + [VMEM] * 5 + [HBM] * 2,
        [(HBM, (2 * WIN, COLS), BF16), (VMEM, (2, WIN, KV), F32), (VMEM, (2, WIN, KV), BF16)],
        [pltpu.VMEM((WIN, COLS), BF16), pltpu.VMEM(PACKED_FAR, BF16), pltpu.VMEM(PACKED_FAR, BF16), DMA((HK,)), DMA((2 * FAR,))],
        SMALL,
        parent, branch, q, d, keys, low_last, ds_last, low, ds,
    )


def late_grads(length, q_last, d_last, k, own, lo, mid, hi, low_last, ds_last, q, d, low, ds, dq):
    return call(
        late_grads_kernel,
        "late_grads",
        [SMEM] + [VMEM] * 9 + [HBM] * 5,
        [(HBM, (2 * WIN, COLS), BF16), (RESULT, (2 * WIN, KV), BF16), (RESULT, (2 * WIN, KV), BF16)],
        [pltpu.VMEM((WIN, COLS), BF16)] * 3
        + [pltpu.VMEM(PACKED, BF16)] * 2
        + [DMA((HK,)), DMA((2 * HK,)), DMA((2 * HK,))],
        SMALL,
        length, q_last, d_last, k, own, lo, mid, hi, low_last, ds_last, q, d, low, ds, dq,
        aliases={14: 0},
    )


def add_up(rows, copies):
    return call(add_up_kernel, "add_up", [VMEM], [(VMEM, (copies, WIN), F32)], [], cost(100, 100), rows)[0]


def sent(rows, levels_on, by):
    levels, branches = lax.axis_size("ctx"), lax.axis_size("expert")
    pairs = [
        (level * branches + b, (level + levels_on) * branches + b + by)
        for level in range(levels)
        for b in range(branches)
        if 0 <= level + levels_on < levels and 0 <= b + by < branches
    ]
    return lax.ppermute(rows, ("ctx", "expert"), pairs)


def shards(query_rows, key_rows, value_rows, output_grad, sink_logits, parent_branch, segment_length):
    q = query_rows[0, 0, 0]
    k = key_rows[0, 0, 0]
    v = value_rows[0, 0, 0]
    d = output_grad[0, 0, 0]
    branch = lax.axis_index("expert").astype(jnp.int32).reshape(1)
    level = lax.axis_index("ctx").astype(jnp.int32).reshape(1)
    plane = lax.axis_size("dp") * lax.axis_size("ctx")
    experts = lax.axis_size("expert")

    k, v, tail, q_first, d_first, sink_rows = load(segment_length, sink_logits, k, v, q, d)
    length = segment_length
    mid, lo, hi = (sent(tail, 1, by) for by in (0, 1, -1))
    q_e, d_e, q_l3, d_l3, low_l, ds_l, low_l3, ds_l3, late_sink = late_rows(length, sink_rows, k, v, q_first, d_first, q, d)
    late_sink, parent = lax.optimization_barrier((late_sink, parent_branch))
    low_e, ds_e, low_e3, ds_e3, keys, sinks = early_rows(parent, branch, level, sink_rows, q_e, d_e, k, v, lo, mid, hi, late_sink, experts)

    column = lax.all_to_all(sinks, "expert", 0, 0, tiled=True)
    dq, early_own, tail = early_grads(parent, branch, q_e, d_e, keys, low_e3, ds_e3, low_e, ds_e)
    mid, lo, hi = (sent(tail, -1, by) for by in (0, 1, -1))
    everywhere = lax.all_to_all(add_up(column, plane), ("dp", "ctx"), 0, 0, tiled=True)
    dq, dk, dv = late_grads(length, q_l3, d_l3, k, early_own, lo, mid, hi, low_l3, ds_l3, q, d, low_l, ds_l, dq)
    everywhere, dk = lax.optimization_barrier((everywhere, dk))
    sink_grad = jnp.sum(everywhere, axis=0)[:HQ]
    return dq[None, None, None], dk[None, None, None], dv[None, None, None], sink_grad


def solution(mesh):
    part = P("dp", "ctx", "expert", None, None)
    scalar = P("dp", "ctx", "expert")
    return jax.shard_map(
        shards,
        mesh=mesh,
        in_specs=(part, part, part, part, P(), scalar, scalar),
        out_specs=(part, part, part, P()),
        check_vma=False,
    )
```
